256 devices in a mesh: grp: 32 (over x, y, z_lo), sec: 8 (over z_hi, core).
Axes of the slice: x: 4, y: 4, z: 8 (z_hi: 4, z_lo: 2; z = z_hi * 2 + z_lo), core: 2. Of those that a mesh axis runs over, the one named last changes fastest.
Arguments:
- coefficients: bfloat16 [65536, 4096], P('sec', 'grp'), may hold values from -0.1875 to 0.1875
- energy_gaps: float32 [4096], P('grp'), may hold values from 0.1 to 10
- metric_blocks: bfloat16 [512, 2, 128, 128], P('sec'), as said below
- metric_index: int32 [512, 2], P('sec'), may hold values from -1 to 511, as said below
- coulomb_blocks: bfloat16 [512, 2, 128, 128], P('sec'), as said below
- coulomb_index: int32 [512, 2], P('sec'), may hold values from -1 to 511, as said below
Outputs:
- response_tiles: float32 [8, 8192, 256], P('sec', 'grp')
The draws below stay inside these ranges and needn't reach their ends.
Inputs may be any that keep to these rules, and one draw needn't show every extreme that they name: `metric_index`: slot 0 of block row r is r itself; every other live slot names a block within 8 blocks of r, counted periodically over 512 blocks; padded slots hold -1 and some slot is padded; in the first block row of each run of 64 blocks every other slot is live and names a block below it, in the last one every other slot is live and names a block above it. `coulomb_index`: slot 0 of block row r is r itself; every other live slot names a block within 8 blocks of r, counted periodically over 512 blocks; padded slots hold -1 and some slot is padded; in the first block row of each run of 64 blocks every other slot is live and names a block below it, in the last one every other slot is live and names a block above it. `metric_blocks`: padded slots hold arbitrary blocks. `coulomb_blocks`: padded slots hold arbitrary blocks.
All inputs are finite; a program needn't handle non-finite values.
Results may differ from the reference program's by a relative error of at most 0.0054.
Values may be sent and summed in bfloat16 or wider, within the bound.
No kernel may reach another device: no remote copies, remote signals or barrier semaphores. Data moves between devices by JAX's collectives and lax.ppermute only.
A program may use at most 64 MiB of HBM per device.

```python
import math
import jax
import jax.numpy as jnp
from jax import lax

BS = 128
RB_DEV = 64
REACH = 8
S_SLOTS = 2
V_SLOTS = 2
CB = 128
QC = 256
NBLK = 512
NAUX = 65536
PAIRS = 4096
N_SEC = 8


def build_blocks(noise, slots, spread):
    eye_block = jnp.eye(BS, dtype=jnp.float32)
    first_slot = (jnp.arange(slots) == 0).astype(jnp.float32)[None, :, None, None]
    return noise * (spread / BS ** 0.5) + first_slot * eye_block[None, None, :, :]


def build_index(key, slots):
    key_mag, key_sign, key_live = jax.random.split(key, 3)
    rows_all = jnp.arange(NBLK, dtype=jnp.int32)
    local_pos = rows_all % RB_DEV
    lower_edge = (local_pos == 0)[:, None]
    upper_edge = (local_pos == RB_DEV - 1)[:, None]
    magnitude = jax.random.randint(key_mag, (NBLK, slots - 1), 1, REACH + 1)
    direction = jax.random.randint(key_sign, (NBLK, slots - 1), 0, 2) * 2 - 1
    direction = jnp.where(lower_edge, -1, jnp.where(upper_edge, 1, direction))
    others = (rows_all[:, None] + magnitude * direction) % NBLK
    live_slots = jax.random.randint(key_live, (NBLK, slots - 1), 0, 3) > 0
    live_slots = live_slots.at[2].set(False).at[1].set(True)
    live_slots = jnp.logical_or(live_slots, jnp.logical_or(lower_edge, upper_edge))
    others = jnp.where(live_slots, others, -1)
    return jnp.concatenate([rows_all[:, None], others], axis=1).astype(jnp.int32)


def draw_metric_index(key, part):
    key = jax.random.fold_in(key, 11)
    return build_index(key, S_SLOTS)


def draw_coulomb_index(key, part):
    key = jax.random.fold_in(key, 13)
    return build_index(key, V_SLOTS)


def draw_metric_blocks(key, part):
    key = jax.random.fold_in(key, 17)
    key_noise = jax.random.fold_in(key, 0)
    shape = (NBLK, S_SLOTS, BS, BS)
    noise = jax.random.normal(key_noise, shape, jnp.float32)
    return build_blocks(noise, S_SLOTS, 0.5).astype(jnp.bfloat16)


def draw_coulomb_blocks(key, part):
    key = jax.random.fold_in(key, 19)
    key_noise = jax.random.fold_in(key, 0)
    shape = (NBLK, V_SLOTS, BS, BS)
    noise = jax.random.normal(key_noise, shape, jnp.float32)
    return build_blocks(noise, V_SLOTS, 0.6).astype(jnp.bfloat16)


def spiked(values, rng, source, target, blocks, factor):
    def block_of(position):
        return (jnp.arange(values.shape[position]) // (values.shape[position] // blocks)).reshape((-1,) + (1,) * (values.ndim - 1 - position))

    first = jax.random.permutation(rng, blocks)[block_of(target)]
    far = (block_of(target) + blocks // 2) % blocks
    return jnp.where((block_of(source) == first) | (block_of(source) == far), factor * values, values)


def block_levels(own_key, shape, shards, low, top_value):
    factor_of = 1.0
    for dim, shards_of in shards:
        steps = jax.random.uniform(jax.random.fold_in(jax.random.fold_in(own_key, 6), dim), (shards_of,), jnp.float32, low / len(shards), top_value / len(shards))
        factor_of = factor_of * jnp.repeat(jnp.exp(steps), shape[dim] // shards_of).reshape((-1,) + (1,) * (len(shape) - 1 - dim))
    return factor_of


def bell_draw_with(rng, dims, deviation, bound, cuts, heavy, kind=jnp.bfloat16):
    values = deviation * jax.random.normal(rng, dims, jnp.float32)
    if cuts:
        values = values * block_levels(rng, dims, cuts, -0.22, 0.18)
    return jnp.clip(spiked(values, jax.random.fold_in(rng, 3), *heavy), -bound, bound).astype(kind)


def setup_inputs(seed: int = 0) -> dict:
    arg_keys = jax.random.split(jax.random.key(seed), 7)
    return {
        "coefficients": bell_draw_with(arg_keys[0], (NAUX, PAIRS), PAIRS ** -0.5, 0.1875, ((0, 8), (1, 32)), (1, 0, 32, 2.75)),
        "energy_gaps": jnp.clip(jnp.exp(math.log(10.0) - 4.6051702 * jax.random.uniform(arg_keys[1], (PAIRS,), jnp.float32) ** block_levels(arg_keys[1], (PAIRS,), ((0, 32),), -0.2, 0.2)), 0.1, 10.0),
        "metric_blocks": draw_metric_blocks(jax.random.fold_in(arg_keys[6], 71), 0),
        "metric_index": draw_metric_index(jax.random.fold_in(arg_keys[6], 71), 0),
        "coulomb_blocks": draw_coulomb_blocks(jax.random.fold_in(arg_keys[6], 71), 0),
        "coulomb_index": draw_coulomb_index(jax.random.fold_in(arg_keys[6], 71), 0),
    }


frequency_sq = 1.0


def apply_operator(blocks, index, field):
    stacked = field.reshape(NBLK, BS, -1).astype(jnp.float32)
    chosen = stacked[jnp.maximum(index, 0)]
    result = jnp.einsum("rkab,rkbc->rac", blocks, chosen)
    return result.reshape(NBLK * BS, -1).astype(jnp.bfloat16)


def masked_blocks(blocks, index):
    live_slots = (index >= 0)[:, :, None, None]
    return jnp.where(live_slots, blocks.astype(jnp.float32), jnp.float32(0.0))


def reference(coefficients, energy_gaps, metric_blocks, metric_index, coulomb_blocks, coulomb_index):
    metric = masked_blocks(metric_blocks, metric_index)
    coulomb = masked_blocks(coulomb_blocks, coulomb_index)
    section_rows = RB_DEV * BS
    pair_weight = 4.0 * energy_gaps / (energy_gaps * energy_gaps + frequency_sq)

    def one_batch(tiles, block_number):
        first_col = (block_number * CB).astype(jnp.int32)
        field = lax.dynamic_slice_in_dim(coefficients, first_col, CB, 1)
        weight_part = lax.dynamic_slice_in_dim(pair_weight, first_col, CB, 0)
        first = apply_operator(metric, metric_index, field)
        second = apply_operator(coulomb, coulomb_index, first)
        btensor = apply_operator(metric, metric_index, second)
        sections = btensor.reshape(N_SEC, section_rows, CB)
        weighted = (sections[:, :QC, :].astype(jnp.float32) * weight_part[None, None, :]).astype(jnp.bfloat16)
        tiles = tiles + jnp.einsum("srp,sqp->srq", sections.astype(jnp.float32), weighted.astype(jnp.float32))
        return tiles, None

    start_tiles = jnp.zeros((N_SEC, section_rows, QC), jnp.float32)
    numbers = jnp.arange(PAIRS // CB, dtype=jnp.int32)
    tiles, unused = lax.scan(one_batch, start_tiles, numbers)
    return tiles
```

```python
import functools

import jax
import jax.numpy as jnp
from jax import lax
from jax.experimental import pallas as pl
from jax.experimental.pallas import tpu as pltpu
from jax.sharding import PartitionSpec as P

BS = 128
ROWS = 64
REACH = 8
NBLK = 512
QC = 256
NX, NY, NZ = 4, 4, 2

frequency_sq = 1.0

VMEM = pl.BlockSpec(memory_space=pltpu.VMEM)
SMEM = pl.BlockSpec(memory_space=pltpu.SMEM)
ANY = pl.BlockSpec(memory_space=pl.ANY)
BF = jnp.bfloat16
F32 = jnp.float32


def blocks_of(count):
    return jax.ShapeDtypeStruct((count, BS, BS), BF)


def params(mib):
    return pltpu.CompilerParams(vmem_limit_bytes=mib * 2**20)


def cost(row_ops, nbytes):
    return pl.CostEstimate(
        flops=row_ops * 4 * BS**3, bytes_accessed=nbytes, transcendentals=0
    )


def coords():
    grp = lax.axis_index("grp")
    return grp // (NY * NZ), (grp // NZ) % NY, grp % NZ


def neighbour(index_ref, row):
    named = index_ref[1, row]
    distance = named - (lax.axis_index("sec") * ROWS + row)
    distance = jnp.where(distance >= NBLK // 2, distance - NBLK, distance)
    distance = jnp.where(distance < -(NBLK // 2), distance + NBLK, distance)
    live = named >= 0
    return jnp.where(live, row + distance, row), live


def row_product(x, field_ref, base, row, index_ref):
    other, live = neighbour(index_ref, row)
    own = field_ref[row - base]
    far = jnp.where(live, field_ref[other - base], jnp.zeros((BS, BS), BF))
    return jnp.dot(
        jnp.concatenate([x[0], x[1]], axis=1),
        jnp.concatenate([own, far], axis=0),
        preferred_element_type=F32,
    ).astype(BF)


def rows_loop(first, count, body):
    def step(k, carry):
        body(first + k)
        return carry

    lax.fori_loop(0, count, step, 0, unroll=4)


def layer_start(layer, y):
    low, high = 8 * (4 - layer), 64 - 8 * (4 - layer) - 8
    if layer % 2 == 0:
        return jnp.where(y < 2, low + 4 * y, high + 4 * (y - 2))
    return jnp.where(y < 2, high + 4 * y, low + 4 * (y - 2))


def layer_rows(layer, outs, body):
    _, y, _ = coords()
    for step in range(NY):
        start = layer_start(layer, (y + step) % NY)
        for k in range(4):
            outs[step][k] = body(start + k)


def inner_kernel(s_index, v_index, c_hbm, s_hbm, v_hbm, first, second, b0, b1, b2, b3, c, s, v, sems):
    copies = [
        pltpu.make_async_copy(c_hbm, c, sems.at[0]),
        pltpu.make_async_copy(s_hbm.at[pl.ds(8, 48)], s, sems.at[1]),
        pltpu.make_async_copy(v_hbm.at[pl.ds(16, 32)], v, sems.at[2]),
    ]
    for copy in copies:
        copy.start()
    copies[0].wait()
    copies[1].wait()

    def one(row):
        first[row - 8] = row_product(s[row - 8], c, 0, row, s_index)

    rows_loop(8, 48, one)
    copies[2].wait()

    def two(row):
        second[row - 16] = row_product(v[row - 16], first, 8, row, v_index)

    rows_loop(16, 32, two)
    layer_rows(1, (b0, b1, b2, b3), lambda row: row_product(s[row - 8], second, 16, row, s_index))


def inner(s_index, v_index, c, s, v):
    return pl.pallas_call(
        inner_kernel,
        out_shape=[blocks_of(48), blocks_of(32)] + [blocks_of(4)] * 4,
        in_specs=[SMEM, SMEM, ANY, ANY, ANY],
        out_specs=[VMEM] * 6,
        scratch_shapes=[
            pltpu.VMEM((64, BS, BS), BF),
            pltpu.VMEM((48, 2, BS, BS), BF),
            pltpu.VMEM((32, 2, BS, BS), BF),
            pltpu.SemaphoreType.DMA((3,)),
        ],
        compiler_params=params(24),
        cost_estimate=cost(96, 14 * 2**20),
    )(s_index, v_index, c, s, v)


def edge_rows(index, low_halo, low, high, high_halo, x_low, x_high, ext, emit):
    ext[0:8] = low_halo[...]
    ext[8:24] = low[...]
    for k in range(8):
        emit(0, k, row_product(x_low[k], ext, -8, k, index))
    ext[0:16] = high[...]
    ext[16:24] = high_halo[...]
    for k in range(8):
        emit(1, k, row_product(x_high[k], ext, 48, 56 + k, index))


def edge_specs(low_block, high_block, low_at, high_at):
    return [
        SMEM,
        VMEM,
        VMEM,
        pl.BlockSpec((low_block, BS, BS), lambda i: (low_at, 0, 0)),
        pl.BlockSpec((high_block, BS, BS), lambda i: (high_at, 0, 0)),
        pl.BlockSpec((8, 2, BS, BS), lambda i: (0, 0, 0, 0)),
        pl.BlockSpec((8, 2, BS, BS), lambda i: (7, 0, 0, 0)),
    ]


def first_edges_kernel(index, low_halo, high_halo, low, high, x_low, x_high, head, tail, ext):
    def emit(side, k, value):
        (head, tail)[side][k] = value

    edge_rows(index, low_halo, low, high, high_halo, x_low, x_high, ext, emit)


def first_edges(index, low_halo, high_halo, field, x):
    return pl.pallas_call(
        first_edges_kernel,
        grid=(1,),
        out_shape=[blocks_of(8)] * 2,
        in_specs=edge_specs(16, 16, 0, 3),
        out_specs=[VMEM] * 2,
        scratch_shapes=[pltpu.VMEM((24, BS, BS), BF)],
        compiler_params=params(16),
        cost_estimate=cost(16, 4 * 2**20),
    )(index, low_halo, high_halo, field, field, x, x)


def middle_kernel(
    s_index, v_index, head, tail, first, second, v_low, v_high, s_low, s_high,
    low_out, high_out, b0, b1, b2, b3, f_low, f_high, e,
):
    f_low[0:8] = head[...]
    f_low[8:24] = first[0:16]
    f_high[0:16] = first[32:48]
    f_high[16:24] = tail[...]
    for k in range(8):
        low_out[k] = row_product(v_low[k], f_low, 0, 8 + k, v_index)
        high_out[k] = row_product(v_high[k], f_high, 40, 48 + k, v_index)
    e[0:8] = low_out[...]
    e[8:40] = second[...]
    e[40:48] = high_out[...]

    def body(row):
        x = jnp.where(row < 32, s_low[row % 8], s_high[row % 8])
        return row_product(x, e, 8, row, s_index)

    layer_rows(2, (b0, b1, b2, b3), body)


def middle(s_index, v_index, head, tail, first, second, v, s):
    def rows_at(at):
        return pl.BlockSpec((8, 2, BS, BS), lambda i: (at, 0, 0, 0))

    return pl.pallas_call(
        middle_kernel,
        grid=(1,),
        out_shape=[blocks_of(8)] * 2 + [blocks_of(4)] * 4,
        in_specs=[SMEM, SMEM] + [VMEM] * 4 + [rows_at(1), rows_at(6), rows_at(2), rows_at(5)],
        out_specs=[VMEM] * 6,
        scratch_shapes=[
            pltpu.VMEM((24, BS, BS), BF),
            pltpu.VMEM((24, BS, BS), BF),
            pltpu.VMEM((48, BS, BS), BF),
        ],
        compiler_params=params(24),
        cost_estimate=cost(32, 8 * 2**20),
    )(s_index, v_index, head, tail, first, second, v, v, s, s)


def second_edges_kernel(
    index, low_halo, high_halo, head, tail, first_low, first_high, x_low, x_high,
    out_head, out_tail, ext,
):
    ext[0:8] = low_halo[...]
    ext[8:16] = head[...]
    ext[16:24] = first_low[...]
    for k in range(8):
        out_head[k] = row_product(x_low[k], ext, -8, k, index)
    ext[0:8] = first_high[...]
    ext[8:16] = tail[...]
    ext[16:24] = high_halo[...]
    for k in range(8):
        out_tail[k] = row_product(x_high[k], ext, 48, 56 + k, index)


def second_edges(index, low_halo, high_halo, head, tail, first, x):
    return pl.pallas_call(
        second_edges_kernel,
        grid=(1,),
        out_shape=[blocks_of(8)] * 2,
        in_specs=[SMEM] + [VMEM] * 4 + edge_specs(8, 8, 0, 5)[3:],
        out_specs=[VMEM] * 2,
        scratch_shapes=[pltpu.VMEM((24, BS, BS), BF)],
        compiler_params=params(16),
        cost_estimate=cost(16, 4 * 2**20),
    )(index, low_halo, high_halo, head, tail, first, first, x, x)


def outer_kernel(index, head, tail, low, high, second, s_low, s_high, b0, b1, b2, b3, e):
    e[0:8] = head[...]
    e[8:16] = low[...]
    e[16:24] = second[0:8]
    e[24:32] = second[24:32]
    e[32:40] = high[...]
    e[40:48] = tail[...]

    def body(row):
        x = jnp.where(row < 32, s_low[row % 8], s_high[row % 8])
        return row_product(x, e, jnp.where(row < 32, 0, 16), row, index)

    layer_rows(3, (b0, b1, b2, b3), body)


def outer(index, head, tail, low, high, second, s):
    def rows_at(at):
        return pl.BlockSpec((8, 2, BS, BS), lambda i: (at, 0, 0, 0))

    return pl.pallas_call(
        outer_kernel,
        grid=(1,),
        out_shape=[blocks_of(4)] * 4,
        in_specs=[SMEM] + [VMEM] * 5 + [rows_at(1), rows_at(6)],
        out_specs=[VMEM] * 4,
        scratch_shapes=[pltpu.VMEM((48, BS, BS), BF)],
        compiler_params=params(16),
        cost_estimate=cost(16, 4 * 2**20),
    )(index, head, tail, low, high, second, s, s)


def last_kernel(
    index, low_halo, high_halo, head, tail, low, high, s_low, s_high, gaps,
    b0, b1, b2, b3, weighted, e,
):
    e[0:8] = low_halo[...]
    e[8:16] = head[...]
    e[16:24] = low[...]
    e[24:32] = high[...]
    e[32:40] = tail[...]
    e[40:48] = high_halo[...]
    gap = gaps[...]
    weight = 4.0 * gap / (gap * gap + frequency_sq)
    for k in range(2):
        value = row_product(s_low[k], e, -8, k, index)
        weighted[k] = (value.astype(F32) * weight).astype(BF)

    def body(row):
        x = jnp.where(row < 32, s_low[row % 8], s_high[row % 8])
        return row_product(x, e, jnp.where(row < 32, -8, 24), row, index)

    layer_rows(4, (b0, b1, b2, b3), body)


def last(index, low_halo, high_halo, head, tail, low, high, s, gaps):
    def rows_at(at):
        return pl.BlockSpec((8, 2, BS, BS), lambda i: (at, 0, 0, 0))

    return pl.pallas_call(
        last_kernel,
        grid=(1,),
        out_shape=[blocks_of(4)] * 4 + [blocks_of(2)],
        in_specs=[SMEM] + [VMEM] * 6 + [rows_at(0), rows_at(7), VMEM],
        out_specs=[VMEM] * 5,
        scratch_shapes=[pltpu.VMEM((48, BS, BS), BF)],
        compiler_params=params(16),
        cost_estimate=cost(18, 4 * 2**20),
    )(index, low_halo, high_halo, head, tail, low, high, s, s, gaps)


def product_kernel(*refs):
    pieces, w_refs = refs[:16], refs[16:20]
    own, outs, b, w = refs[20], refs[21:28], refs[28], refs[29]
    for layer in range(4):
        for source in range(4):
            b[layer, :, source * BS : (source + 1) * BS] = pieces[layer * 4 + source][...].reshape(4 * BS, BS)
    for source in range(4):
        w[:, source * BS : (source + 1) * BS] = w_refs[source][...].reshape(QC, BS)
    x, y, z = coords()
    for step in range(NX):
        to = (x + step) % NX
        near = jnp.where(to == 2, 0, jnp.where(to == 1, 1, jnp.where(to == 3, 2, 3)))
        away = jnp.where(to == 1, 0, jnp.where(to == 2, 1, jnp.where(to == 0, 2, 3)))
        layer = jnp.where(y < 2, near, away)
        for flip in range(NZ):
            half = (z + flip) % NZ
            tile = lax.dot_general(
                b[layer, pl.ds(pl.multiple_of(half * QC, QC), QC), :],
                w[...],
                (((1,), (1,)), ((), ())),
                preferred_element_type=F32,
            )
            if step == 0 and flip == 0:
                own[...] = tile
            else:
                outs[step * NZ + flip - 1][...] = tile.astype(BF)


def product(pieces, weights):
    tile = jax.ShapeDtypeStruct((QC, QC), BF)
    return pl.pallas_call(
        product_kernel,
        out_shape=[jax.ShapeDtypeStruct((QC, QC), F32)] + [tile] * 7,
        in_specs=[VMEM] * 20,
        out_specs=[VMEM] * 8,
        scratch_shapes=[pltpu.VMEM((4, 4 * BS, 4 * BS), BF), pltpu.VMEM((QC, 4 * BS), BF)],
        compiler_params=params(24),
        cost_estimate=pl.CostEstimate(
            flops=2 * 2048 * 512 * 256, bytes_accessed=8 * 2**20, transcendentals=0
        ),
    )(*pieces, *weights)


def add_kernel(*refs):
    total = refs[0][...]
    for ref in refs[1:8]:
        total += ref[...].astype(F32)
    refs[8][0] = total


def add_up(own, others):
    return pl.pallas_call(
        add_kernel,
        out_shape=jax.ShapeDtypeStruct((1, QC, QC), F32),
        in_specs=[VMEM] * 8,
        out_specs=VMEM,
        compiler_params=params(8),
        cost_estimate=pl.CostEstimate(flops=8 * QC * QC, bytes_accessed=2**20, transcendentals=0),
    )(own, *others)


def grp_shift(value, dx, dy, dz):
    pairs = []
    for x in range(NX):
        for y in range(NY):
            for z in range(NZ):
                to = ((x + dx) % NX * NY + (y + dy) % NY) * NZ + (z + dz) % NZ
                pairs.append(((x * NY + y) * NZ + z, to))
    return lax.ppermute(value, "grp", pairs)


def halo(head, tail):
    count = lax.axis_size("sec")
    up = [(i, (i + 1) % count) for i in range(count)]
    down = [((i + 1) % count, i) for i in range(count)]
    return lax.ppermute(tail, "sec", up), lax.ppermute(head, "sec", down)


def spread_y(parts):
    return [parts[0]] + [grp_shift(parts[d], 0, d, 0) for d in (1, 2, 3)]


def on_device(coefficients, energy_gaps, metric_blocks, metric_index, coulomb_blocks, coulomb_index):
    c = coefficients.reshape(ROWS, BS, BS)
    s, v = metric_blocks, coulomb_blocks
    s_index, v_index = metric_index.T, coulomb_index.T
    gaps = energy_gaps.reshape(1, BS)

    c_low, c_high = halo(c[:8], c[56:])
    first, second, *layer1 = inner(s_index, v_index, c, s, v)
    layer1 = spread_y(layer1)
    f_head, f_tail = first_edges(s_index, c_low, c_high, c, s)
    f_low, f_high = halo(f_head, f_tail)
    e_low, e_high, *layer2 = middle(s_index, v_index, f_head, f_tail, first, second, v, s)
    layer2 = spread_y(layer2)
    e_head, e_tail = second_edges(v_index, f_low, f_high, f_head, f_tail, first, v)
    g_low, g_high = halo(e_head, e_tail)
    layer3 = outer(s_index, e_head, e_tail, e_low, e_high, second, s)
    layer3 = spread_y(layer3)
    *layer4, weighted = last(s_index, g_low, g_high, e_head, e_tail, e_low, e_high, s, gaps)
    weights = spread_y([weighted] * 4)
    layer4 = spread_y(layer4)
    own, *others = product([*layer1, *layer2, *layer3, *layer4], weights)
    sent = [
        grp_shift(others[step * NZ + flip - 1], step, 0, flip)
        for step in range(NX)
        for flip in range(NZ)
        if step or flip
    ]
    return add_up(own, sent)


def solution(mesh):
    placed = (
        P("sec", "grp"),
        P("grp"),
        P("sec", None, None, None),
        P("sec", None),
        P("sec", None, None, None),
        P("sec", None),
    )
    return jax.shard_map(
        on_device, mesh=mesh, in_specs=placed, out_specs=P("sec", "grp", None), check_vma=False
    )
```

```python
import jax
import jax.numpy as jnp
from jax import lax
from jax.experimental import pallas as pl
from jax.experimental.pallas import tpu as pltpu
from jax.sharding import PartitionSpec as P

BS = 128
ROWS = 64
REACH = 8
NBLK = 512
QC = 256
NX, NY, NZ = 4, 4, 2

frequency_sq = 1.0

VMEM = pl.BlockSpec(memory_space=pltpu.VMEM)
SMEM = pl.BlockSpec(memory_space=pltpu.SMEM)
HBM = pl.BlockSpec(memory_space=pltpu.HBM)
BF = jnp.bfloat16
F32 = jnp.float32


def blocks_of(count):
    return jax.ShapeDtypeStruct((count, BS, BS), BF)


def params(mib):
    return pltpu.CompilerParams(vmem_limit_bytes=mib * 2**20)


def cost(row_ops, nbytes):
    return pl.CostEstimate(
        flops=row_ops * 4 * BS**3, bytes_accessed=nbytes, transcendentals=0
    )


def coords():
    grp = lax.axis_index("grp")
    return grp // (NY * NZ), (grp // NZ) % NY, grp % NZ


def positions(index, first_row):
    rows = lax.broadcasted_iota(jnp.int32, (ROWS,), 0)
    distance = index[:, 1] - (first_row + rows)
    distance = jnp.where(distance >= NBLK // 2, distance - NBLK, distance)
    distance = jnp.where(distance < -(NBLK // 2), distance + NBLK, distance)
    return jnp.where(index[:, 1] >= 0, rows + distance, -NBLK)


def neighbour(index_ref, row):
    other = index_ref[row]
    live = other > -NBLK
    return jnp.where(live, other, row), live


def row_product(x, field_ref, base, row, index_ref):
    other, live = neighbour(index_ref, row)
    own = field_ref[row - base]
    far = jnp.where(live, field_ref[other - base], jnp.zeros((BS, BS), BF))
    return jnp.dot(
        jnp.concatenate([x[0], x[1]], axis=1),
        jnp.concatenate([own, far], axis=0),
        preferred_element_type=F32,
    ).astype(BF)


def rows_loop(first, count, body):
    def step(k, carry):
        body(first + k)
        return carry

    lax.fori_loop(0, count, step, 0, unroll=16)


def layer_start(layer, y):
    low, high = 8 * (4 - layer), 64 - 8 * (4 - layer) - 8
    if layer % 2 == 0:
        return jnp.where(y < 2, low + 4 * y, high + 4 * (y - 2))
    return jnp.where(y < 2, high + 4 * y, low + 4 * (y - 2))


def stored_slot(layer, start):
    low = 8 * (4 - layer)
    return jnp.where(start < 32, start - low, start + low - 48)


def inner_kernel(
    s_index, v_index, c_hbm, s_hbm, v_hbm,
    first, second, layer1, c_edge, s_edge, v_edge, v_mid, s_mid, s_out,
    c, s, v, sems,
):
    def load(k, source, target, at, to, count):
        return pltpu.make_async_copy(source.at[pl.ds(at, count)], target.at[pl.ds(to, count)], sems.at[k])

    copies = [
        load(0, c_hbm, c, 0, 0, 64),
        load(1, s_hbm, s, 8, 0, 16),
        load(2, s_hbm, s, 24, 16, 16),
        load(3, s_hbm, s, 40, 32, 16),
        load(4, v_hbm, v, 16, 0, 32),
        load(5, c_hbm, c_edge, 0, 0, 16),
        load(6, c_hbm, c_edge, 48, 16, 16),
    ]
    pieces = ((s_hbm, s_edge, 0), (v_hbm, v_edge, 0), (v_hbm, v_mid, 8), (s_hbm, s_mid, 16), (s_hbm, s_out, 8))
    for source, target, at in pieces:
        copies.append(load(len(copies), source, target, at, 0, 8))
        copies.append(load(len(copies), source, target, 56 - at, 8, 8))
    for copy in copies[:5]:
        copy.start()
    copies[0].wait()

    def one(row):
        first[row - 8] = row_product(s[row - 8], c, 0, row, s_index)

    for k in range(3):
        copies[1 + k].wait()
        rows_loop(8 + 16 * k, 16, one)
        if k == 0:
            for copy in copies[5:]:
                copy.start()
    copies[4].wait()

    def two(row):
        second[row - 16] = row_product(v[row - 16], first, 8, row, v_index)

    rows_loop(16, 32, two)
    _, y, _ = coords()
    for step in range(NY):
        start = layer_start(1, (y + step) % NY)
        for k in range(4):
            layer1[4 * step + k] = row_product(s[start + k - 8], second, 16, start + k, s_index)
    for copy in copies[5:]:
        copy.wait()


def inner(s_index, v_index, c, s, v):
    stored = jax.ShapeDtypeStruct((16, 2, BS, BS), BF)
    return pl.pallas_call(
        inner_kernel,
        out_shape=[blocks_of(48), blocks_of(32), blocks_of(16), blocks_of(32)] + [stored] * 5,
        in_specs=[SMEM, SMEM, HBM, HBM, HBM],
        out_specs=[VMEM] * 9,
        scratch_shapes=[
            pltpu.VMEM((64, BS, BS), BF),
            pltpu.VMEM((48, 2, BS, BS), BF),
            pltpu.VMEM((32, 2, BS, BS), BF),
            pltpu.SemaphoreType.DMA((17,)),
        ],
        compiler_params=params(44),
        cost_estimate=cost(96, 14 * 2**20),
    )(s_index, v_index, c, s, v)


def place(ref, far, near, head_at, tail_at):
    odd = lax.axis_index("sec") % 2
    ref[pl.ds(jnp.where(odd == 1, tail_at, head_at), 8)] = far[...]
    ref[pl.ds(jnp.where(odd == 1, head_at, tail_at), 8)] = near[...]


def edge_rows(index, ext, x, far, near):
    odd = lax.axis_index("sec") % 2
    for out, high in ((far, odd), (near, 1 - odd)):
        for k in range(8):
            out[k] = row_product(x[8 * high + k], ext, 32 * high - 8, 56 * high + k, index)


def first_edges_kernel(index, far_halo, near_halo, c, x, far, near, ext):
    place(ext, far_halo, near_halo, 0, 40)
    ext[8:40] = c[...]
    edge_rows(index, ext, x, far, near)


def second_edges_kernel(
    index, far_halo, near_halo, f_far, f_near, first, x, after, far, near, ext
):
    place(ext, far_halo, near_halo, 0, 40)
    place(ext, f_far, f_near, 8, 32)
    ext[16:24] = first[0:8]
    ext[24:32] = first[40:48]
    edge_rows(index, ext, x, far, near)


def edges(kernel, *operands):
    return pl.pallas_call(
        kernel,
        out_shape=[blocks_of(8)] * 2,
        in_specs=[SMEM] + [VMEM] * (len(operands) - 1),
        out_specs=[VMEM] * 2,
        scratch_shapes=[pltpu.VMEM((48, BS, BS), BF)],
        compiler_params=params(4),
        cost_estimate=cost(16, 3 * 2**20),
    )(*operands)


def middle_kernel(
    s_index, v_index, far, near, first, second, layer1, v, s, low_out, high_out, b0, b1, b2, b3, f, e
):
    place(f, far, near, 0, 40)
    f[8:24] = first[0:16]
    f[24:40] = first[32:48]
    for k in range(8):
        low_out[k] = row_product(v[k], f, 0, 8 + k, v_index)
        high_out[k] = row_product(v[8 + k], f, 16, 48 + k, v_index)
    e[0:8] = low_out[...]
    e[8:40] = second[...]
    e[40:48] = high_out[...]
    _, y, _ = coords()
    for step, out in enumerate((b0, b1, b2, b3)):
        out[0:4] = layer1[4 * step : 4 * step + 4]
        start = layer_start(2, (y + step) % NY)
        slot = stored_slot(2, start)
        for k in range(4):
            out[4 + k] = row_product(s[slot + k], e, 8, start + k, s_index)


def middle(*operands):
    return pl.pallas_call(
        middle_kernel,
        out_shape=[blocks_of(8)] * 6,
        in_specs=[SMEM, SMEM] + [VMEM] * 7,
        out_specs=[VMEM] * 6,
        scratch_shapes=[pltpu.VMEM((48, BS, BS), BF), pltpu.VMEM((48, BS, BS), BF)],
        compiler_params=params(4),
        cost_estimate=cost(32, 8 * 2**20),
    )(*operands)


def outer_kernel(index, far, near, low, high, second, s, layer3, e):
    place(e, far, near, 0, 40)
    e[8:16] = low[...]
    e[16:24] = second[0:8]
    e[24:32] = second[24:32]
    e[32:40] = high[...]
    _, y, _ = coords()
    for step in range(NY):
        start = layer_start(3, (y + step) % NY)
        slot = stored_slot(3, start)
        base = jnp.where(start < 32, 0, 16)
        for k in range(4):
            layer3[4 * step + k] = row_product(s[slot + k], e, base, start + k, index)


def outer(*operands):
    return pl.pallas_call(
        outer_kernel,
        out_shape=blocks_of(16),
        in_specs=[SMEM] + [VMEM] * 6,
        out_specs=VMEM,
        scratch_shapes=[pltpu.VMEM((48, BS, BS), BF)],
        compiler_params=params(4),
        cost_estimate=cost(16, 4 * 2**20),
    )(*operands)


def last_kernel(
    index, far_halo, near_halo, far, near, low, high, s, gaps, layer3, after1, after2, after3,
    b0, b1, b2, b3, e,
):
    place(e, far_halo, near_halo, 0, 40)
    place(e, far, near, 8, 32)
    e[16:24] = low[...]
    e[24:32] = high[...]
    gap = gaps[...]
    weight = 4.0 * gap / (gap * gap + frequency_sq)
    _, y, _ = coords()
    for k in range(2):
        value = row_product(s[k], e, -8, k, index)
        weighted = (value.astype(F32) * weight).astype(BF)
        for out in (b0, b1, b2, b3):
            out[8 + k] = weighted
    for step, out in enumerate((b0, b1, b2, b3)):
        out[0:4] = layer3[4 * step : 4 * step + 4]
        start = layer_start(4, (y + step) % NY)
        slot = stored_slot(4, start)
        base = jnp.where(start < 32, -8, 24)
        for k in range(4):
            out[4 + k] = row_product(s[slot + k], e, base, start + k, index)


def last(*operands):
    return pl.pallas_call(
        last_kernel,
        out_shape=[blocks_of(10)] * 4,
        in_specs=[SMEM] + [VMEM] * 12,
        out_specs=[VMEM] * 4,
        scratch_shapes=[pltpu.VMEM((48, BS, BS), BF)],
        compiler_params=params(4),
        cost_estimate=cost(18, 4 * 2**20),
    )(*operands)


def product_kernel(*refs):
    inside, outside = refs[:4], refs[4:8]
    own, outs, b, w = refs[8], refs[9:16], refs[16], refs[17]
    for source in range(4):
        lanes = slice(source * BS, (source + 1) * BS)
        for k in range(2):
            b[k, :, lanes] = inside[source][4 * k : 4 * k + 4].reshape(4 * BS, BS)
            b[2 + k, :, lanes] = outside[source][4 * k : 4 * k + 4].reshape(4 * BS, BS)
        w[:, lanes] = outside[source][8:10].reshape(QC, BS)
    x, y, z = coords()
    for step in range(NX):
        to = x ^ step
        near = jnp.where(to == 2, 0, jnp.where(to == 1, 1, jnp.where(to == 3, 2, 3)))
        away = jnp.where(to == 1, 0, jnp.where(to == 2, 1, jnp.where(to == 0, 2, 3)))
        layer = jnp.where(y < 2, near, away)
        for flip in range(NZ):
            half = z ^ flip
            tile = lax.dot_general(
                b[layer, pl.ds(pl.multiple_of(half * QC, QC), QC), :],
                w[...],
                (((1,), (1,)), ((), ())),
                preferred_element_type=F32,
            )
            if step == 0 and flip == 0:
                own[...] = tile
            else:
                outs[step * NZ + flip - 1][...] = tile.astype(BF)


def product(*operands):
    tile = jax.ShapeDtypeStruct((QC, QC), BF)
    return pl.pallas_call(
        product_kernel,
        out_shape=[jax.ShapeDtypeStruct((QC, QC), F32)] + [tile] * 7,
        in_specs=[VMEM] * 8,
        out_specs=[VMEM] * 8,
        scratch_shapes=[pltpu.VMEM((4, 4 * BS, 4 * BS), BF), pltpu.VMEM((QC, 4 * BS), BF)],
        compiler_params=params(8),
        cost_estimate=pl.CostEstimate(
            flops=2 * 2048 * 512 * 256, bytes_accessed=8 * 2**20, transcendentals=0
        ),
    )(*operands)


def add_kernel(*refs):
    total = refs[0][...]
    for ref in refs[1:8]:
        total += ref[...].astype(F32)
    refs[8][0] = total


def add_up(own, others):
    return pl.pallas_call(
        add_kernel,
        out_shape=jax.ShapeDtypeStruct((1, QC, QC), F32),
        in_specs=[VMEM] * 8,
        out_specs=VMEM,
        compiler_params=params(8),
        cost_estimate=pl.CostEstimate(flops=8 * QC * QC, bytes_accessed=2**20, transcendentals=0),
    )(own, *others)


def swap(value, dx, dy, dz):
    pairs = []
    for x in range(NX):
        for y in range(NY):
            for z in range(NZ):
                pairs.append(((x * NY + y) * NZ + z, ((x ^ dx) * NY + (y ^ dy)) * NZ + (z ^ dz)))
    return lax.ppermute(value, "grp", pairs)


def halo(far, near):
    count = lax.axis_size("sec")
    far_pairs = [(i, (i + 1 if i % 2 else i - 1) % count) for i in range(count)]
    near_pairs = [(i, i ^ 1) for i in range(count)]
    return lax.ppermute(far, "sec", far_pairs), lax.ppermute(near, "sec", near_pairs)


def spread_y(parts):
    out = [parts[0]]
    for d in range(1, NY):
        pairs = []
        for k in range(NX * NY * NZ):
            x, y, z = k // (NY * NZ), k // NZ % NY, k % NZ
            pairs.append((k, (x * NY + (y + d) % NY) * NZ + z))
        out.append(lax.ppermute(parts[d], "grp", pairs))
    return out


def on_device(coefficients, energy_gaps, metric_blocks, metric_index, coulomb_blocks, coulomb_index):
    c = coefficients.reshape(ROWS, BS, BS)
    s, v = metric_blocks, coulomb_blocks
    first_row = lax.axis_index("sec") * ROWS
    s_index, v_index = positions(metric_index, first_row), positions(coulomb_index, first_row)
    gaps = energy_gaps.reshape(1, BS)

    odd = lax.axis_index("sec") % 2 == 1
    c_far, c_near = halo(jnp.where(odd, c[56:], c[:8]), jnp.where(odd, c[:8], c[56:]))
    first, second, layer1, c_edge, s_edge, v_edge, v_mid, s_mid, s_out = inner(s_index, v_index, c, s, v)
    f_sends = edges(first_edges_kernel, s_index, c_far, c_near, c_edge, s_edge)
    f_halos = halo(*f_sends)
    e_low, e_high, *inside = middle(s_index, v_index, *f_sends, first, second, layer1, v_mid, s_mid)
    inside = spread_y(inside)
    e_sends = edges(second_edges_kernel, v_index, *f_halos, *f_sends, first, v_edge, e_low)
    e_halos = halo(*e_sends)
    layer3 = outer(s_index, *e_sends, e_low, e_high, second, s_out)
    outside = last(
        s_index, *e_halos, *e_sends, e_low, e_high, s_edge, gaps, layer3, *inside[1:]
    )
    outside = spread_y(outside)
    own, *others = product(*inside, *outside)
    sent = [
        swap(others[step * NZ + flip - 1], step, 0, flip)
        for step in range(NX)
        for flip in range(NZ)
        if step or flip
    ]
    return add_up(own, sent)


def solution(mesh):
    placed = (
        P("sec", "grp"),
        P("grp"),
        P("sec", None, None, None),
        P("sec", None),
        P("sec", None, None, None),
        P("sec", None),
    )
    return jax.shard_map(
        on_device, mesh=mesh, in_specs=placed, out_specs=P("sec", "grp", None), check_vma=False
    )
```

```python
import jax
import jax.numpy as jnp
from jax import lax
from jax.experimental import pallas as pl
from jax.experimental.pallas import tpu as pltpu
from jax.sharding import PartitionSpec as P

BS = 128
ROWS = 64
REACH = 8
NBLK = 512
QC = 256
NX, NY, NZ = 4, 4, 2

frequency_sq = 1.0

VMEM = pl.BlockSpec(memory_space=pltpu.VMEM)
SMEM = pl.BlockSpec(memory_space=pltpu.SMEM)
HBM = pl.BlockSpec(memory_space=pltpu.HBM)
BF = jnp.bfloat16
F32 = jnp.float32


def blocks_of(count):
    return jax.ShapeDtypeStruct((count, BS, BS), BF)


def params(mib):
    return pltpu.CompilerParams(vmem_limit_bytes=mib * 2**20)


def cost(row_ops, nbytes):
    return pl.CostEstimate(
        flops=row_ops * 4 * BS**3, bytes_accessed=nbytes, transcendentals=0
    )


def coords():
    grp = lax.axis_index("grp")
    return grp // (NY * NZ), (grp // NZ) % NY, grp % NZ


def positions(index, first_row):
    rows = lax.broadcasted_iota(jnp.int32, (ROWS,), 0)
    distance = index[:, 1] - (first_row + rows)
    distance = jnp.where(distance >= NBLK // 2, distance - NBLK, distance)
    distance = jnp.where(distance < -(NBLK // 2), distance + NBLK, distance)
    return jnp.where(index[:, 1] >= 0, rows + distance, -NBLK)


def neighbour(index_ref, row):
    other = index_ref[row]
    live = other > -NBLK
    return jnp.where(live, other, row), live


def row_product(x, field_ref, base, row, index_ref):
    other, live = neighbour(index_ref, row)
    own = field_ref[row - base]
    far = jnp.where(live, field_ref[other - base], jnp.zeros((BS, BS), BF))
    return jnp.dot(
        jnp.concatenate([x[0], x[1]], axis=1),
        jnp.concatenate([own, far], axis=0),
        preferred_element_type=F32,
    ).astype(BF)


def rows_loop(first, count, body):
    def step(k, carry):
        body(first + k)
        return carry

    lax.fori_loop(0, count, step, 0, unroll=16)


def layer_start(layer, y):
    low, high = 8 * (4 - layer), 64 - 8 * (4 - layer) - 8
    if layer % 2 == 0:
        return jnp.where(y < 2, low + 4 * y, high + 4 * (y - 2))
    return jnp.where(y < 2, high + 4 * y, low + 4 * (y - 2))


def stored_slot(layer, start):
    low = 8 * (4 - layer)
    return jnp.where(start < 32, start - low, start + low - 48)


def inner_kernel(
    s_index, v_index, c_hbm, s_hbm, v_hbm,
    first, second, layer1, c_edge, s_edge, v_edge, v_mid, s_mid, s_out,
    c, s, v, sems,
):
    def load(k, source, target, at, to, count):
        return pltpu.make_async_copy(source.at[pl.ds(at, count)], target.at[pl.ds(to, count)], sems.at[k])

    copies = [
        load(0, c_hbm, c, 0, 0, 64),
        load(1, s_hbm, s, 8, 0, 16),
        load(2, s_hbm, s, 24, 16, 16),
        load(3, s_hbm, s, 40, 32, 16),
        load(4, v_hbm, v, 16, 0, 32),
        load(5, c_hbm, c_edge, 0, 0, 16),
        load(6, c_hbm, c_edge, 48, 16, 16),
    ]
    pieces = ((s_hbm, s_edge, 0), (v_hbm, v_edge, 0), (v_hbm, v_mid, 8), (s_hbm, s_mid, 16), (s_hbm, s_out, 8))
    for source, target, at in pieces:
        copies.append(load(len(copies), source, target, at, 0, 8))
        copies.append(load(len(copies), source, target, 56 - at, 8, 8))
    for copy in copies[:5]:
        copy.start()
    copies[0].wait()

    def one(row):
        first[row - 8] = row_product(s[row - 8], c, 0, row, s_index)

    for k in range(3):
        copies[1 + k].wait()
        rows_loop(8 + 16 * k, 16, one)
        if k == 0:
            for copy in copies[5:]:
                copy.start()
    copies[4].wait()

    def two(row):
        second[row - 16] = row_product(v[row - 16], first, 8, row, v_index)

    rows_loop(16, 32, two)
    _, y, _ = coords()
    for step in range(NY):
        start = layer_start(1, (y + step) % NY)
        for k in range(4):
            layer1[4 * step + k] = row_product(s[start + k - 8], second, 16, start + k, s_index)
    for copy in copies[5:]:
        copy.wait()


def inner(s_index, v_index, c, s, v):
    stored = jax.ShapeDtypeStruct((16, 2, BS, BS), BF)
    return pl.pallas_call(
        inner_kernel,
        out_shape=[blocks_of(48), blocks_of(32), blocks_of(16), blocks_of(32)] + [stored] * 5,
        in_specs=[SMEM, SMEM, HBM, HBM, HBM],
        out_specs=[VMEM] * 9,
        scratch_shapes=[
            pltpu.VMEM((64, BS, BS), BF),
            pltpu.VMEM((48, 2, BS, BS), BF),
            pltpu.VMEM((32, 2, BS, BS), BF),
            pltpu.SemaphoreType.DMA((17,)),
        ],
        compiler_params=params(44),
        cost_estimate=cost(96, 14 * 2**20),
    )(s_index, v_index, c, s, v)


def place(ref, far, near, head_at, tail_at):
    odd = lax.axis_index("sec") % 2
    ref[pl.ds(jnp.where(odd == 1, tail_at, head_at), 8)] = far[...]
    ref[pl.ds(jnp.where(odd == 1, head_at, tail_at), 8)] = near[...]


def edge_rows(index, ext, x, far, near):
    odd = lax.axis_index("sec") % 2
    for out, high in ((far, odd), (near, 1 - odd)):
        for k in range(8):
            out[k] = row_product(x[8 * high + k], ext, 32 * high - 8, 56 * high + k, index)


def first_edges_kernel(index, far_halo, near_halo, c, x, far, near, ext):
    place(ext, far_halo, near_halo, 0, 40)
    ext[8:40] = c[...]
    edge_rows(index, ext, x, far, near)


def second_edges_kernel(
    index, far_halo, near_halo, f_far, f_near, first, x, after, far, near, ext
):
    place(ext, far_halo, near_halo, 0, 40)
    place(ext, f_far, f_near, 8, 32)
    ext[16:24] = first[0:8]
    ext[24:32] = first[40:48]
    edge_rows(index, ext, x, far, near)


def edges(kernel, *operands):
    return pl.pallas_call(
        kernel,
        out_shape=[blocks_of(8)] * 2,
        in_specs=[SMEM] + [VMEM] * (len(operands) - 1),
        out_specs=[VMEM] * 2,
        scratch_shapes=[pltpu.VMEM((48, BS, BS), BF)],
        compiler_params=params(4),
        cost_estimate=cost(16, 3 * 2**20),
    )(*operands)


def middle_kernel(
    s_index, v_index, far, near, first, second, layer1, v, s, low_out, high_out, b0, b1, b2, b3, f, e
):
    place(f, far, near, 0, 40)
    f[8:24] = first[0:16]
    f[24:40] = first[32:48]
    for k in range(8):
        low_out[k] = row_product(v[k], f, 0, 8 + k, v_index)
        high_out[k] = row_product(v[8 + k], f, 16, 48 + k, v_index)
    e[0:8] = low_out[...]
    e[8:40] = second[...]
    e[40:48] = high_out[...]
    _, y, _ = coords()
    for step, out in enumerate((b0, b1, b2, b3)):
        out[0:4] = layer1[4 * step : 4 * step + 4]
        start = layer_start(2, (y + step) % NY)
        slot = stored_slot(2, start)
        for k in range(4):
            out[4 + k] = row_product(s[slot + k], e, 8, start + k, s_index)


def middle(*operands):
    return pl.pallas_call(
        middle_kernel,
        out_shape=[blocks_of(8)] * 6,
        in_specs=[SMEM, SMEM] + [VMEM] * 7,
        out_specs=[VMEM] * 6,
        scratch_shapes=[pltpu.VMEM((48, BS, BS), BF), pltpu.VMEM((48, BS, BS), BF)],
        compiler_params=params(4),
        cost_estimate=cost(32, 8 * 2**20),
    )(*operands)


def outer_kernel(index, far, near, low, high, second, s, layer3, e):
    place(e, far, near, 0, 40)
    e[8:16] = low[...]
    e[16:24] = second[0:8]
    e[24:32] = second[24:32]
    e[32:40] = high[...]
    _, y, _ = coords()
    for step in range(NY):
        start = layer_start(3, (y + step) % NY)
        slot = stored_slot(3, start)
        base = jnp.where(start < 32, 0, 16)
        for k in range(4):
            layer3[4 * step + k] = row_product(s[slot + k], e, base, start + k, index)


def outer(*operands):
    return pl.pallas_call(
        outer_kernel,
        out_shape=blocks_of(16),
        in_specs=[SMEM] + [VMEM] * 6,
        out_specs=VMEM,
        scratch_shapes=[pltpu.VMEM((48, BS, BS), BF)],
        compiler_params=params(4),
        cost_estimate=cost(16, 4 * 2**20),
    )(*operands)


def last_kernel(
    index, far_halo, near_halo, far, near, low, high, s, gaps, layer3, after1, after2, after3,
    b0, b1, b2, b3, e,
):
    place(e, far_halo, near_halo, 0, 40)
    place(e, far, near, 8, 32)
    e[16:24] = low[...]
    e[24:32] = high[...]
    gap = gaps[...]
    weight = 4.0 * gap / (gap * gap + frequency_sq)
    _, y, _ = coords()
    for k in range(2):
        value = row_product(s[k], e, -8, k, index)
        weighted = (value.astype(F32) * weight).astype(BF)
        for out in (b0, b1, b2, b3):
            out[8 + k] = weighted
    for step, out in enumerate((b0, b1, b2, b3)):
        out[0:4] = layer3[4 * step : 4 * step + 4]
        start = layer_start(4, (y + step) % NY)
        slot = stored_slot(4, start)
        base = jnp.where(start < 32, -8, 24)
        for k in range(4):
            out[4 + k] = row_product(s[slot + k], e, base, start + k, index)


def last(*operands):
    return pl.pallas_call(
        last_kernel,
        out_shape=[blocks_of(10)] * 4,
        in_specs=[SMEM] + [VMEM] * 12,
        out_specs=[VMEM] * 4,
        scratch_shapes=[pltpu.VMEM((48, BS, BS), BF)],
        compiler_params=params(4),
        cost_estimate=cost(18, 4 * 2**20),
    )(*operands)


def product_kernel(*refs):
    inside, outside = refs[:4], refs[4:8]
    own, outs, b, w = refs[8], refs[9:16], refs[16], refs[17]
    for source in range(4):
        lanes = slice(source * BS, (source + 1) * BS)
        for k in range(2):
            b[k, :, lanes] = inside[source][4 * k : 4 * k + 4].reshape(4 * BS, BS)
            b[2 + k, :, lanes] = outside[source][4 * k : 4 * k + 4].reshape(4 * BS, BS)
        w[:, lanes] = outside[source][8:10].reshape(QC, BS)
    x, y, z = coords()
    for step in range(NX):
        to = x ^ step
        near = jnp.where(to == 2, 0, jnp.where(to == 1, 1, jnp.where(to == 3, 2, 3)))
        away = jnp.where(to == 1, 0, jnp.where(to == 2, 1, jnp.where(to == 0, 2, 3)))
        layer = jnp.where(y < 2, near, away)
        for flip in range(NZ):
            half = z ^ flip
            tile = lax.dot_general(
                b[layer, pl.ds(pl.multiple_of(half * QC, QC), QC), :],
                w[...],
                (((1,), (1,)), ((), ())),
                preferred_element_type=F32,
            )
            if step == 0 and flip == 0:
                own[...] = tile
            else:
                outs[step * NZ + flip - 1][...] = tile.astype(BF)


def product(*operands):
    tile = jax.ShapeDtypeStruct((QC, QC), BF)
    return pl.pallas_call(
        product_kernel,
        out_shape=[jax.ShapeDtypeStruct((QC, QC), F32)] + [tile] * 7,
        in_specs=[VMEM] * 8,
        out_specs=[VMEM] * 8,
        scratch_shapes=[pltpu.VMEM((4, 4 * BS, 4 * BS), BF), pltpu.VMEM((QC, 4 * BS), BF)],
        compiler_params=params(8),
        cost_estimate=pl.CostEstimate(
            flops=2 * 2048 * 512 * 256, bytes_accessed=8 * 2**20, transcendentals=0
        ),
    )(*operands)


def add_kernel(*refs):
    total = refs[0][...]
    for ref in refs[1:8]:
        total += ref[...].astype(F32)
    refs[8][0] = total


def add_up(own, others):
    return pl.pallas_call(
        add_kernel,
        out_shape=jax.ShapeDtypeStruct((1, QC, QC), F32),
        in_specs=[VMEM] * 8,
        out_specs=VMEM,
        compiler_params=params(8),
        cost_estimate=pl.CostEstimate(flops=8 * QC * QC, bytes_accessed=2**20, transcendentals=0),
    )(own, *others)


def swap(value, dx, dy, dz):
    pairs = []
    for x in range(NX):
        for y in range(NY):
            for z in range(NZ):
                pairs.append(((x * NY + y) * NZ + z, ((x ^ dx) * NY + (y ^ dy)) * NZ + (z ^ dz)))
    return lax.ppermute(value, "grp", pairs)


def halo(far, near):
    count = lax.axis_size("sec")
    far_pairs = [(i, (i + 1 if i % 2 else i - 1) % count) for i in range(count)]
    near_pairs = [(i, i ^ 1) for i in range(count)]
    return lax.ppermute(far, "sec", far_pairs), lax.ppermute(near, "sec", near_pairs)


def spread_y(parts, order=(1, 3, 2)):
    out = {0: parts[0]}
    for d in order:
        pairs = []
        for k in range(NX * NY * NZ):
            x, y, z = k // (NY * NZ), k // NZ % NY, k % NZ
            pairs.append((k, (x * NY + (y + d) % NY) * NZ + z))
        out[d] = lax.ppermute(parts[d], "grp", pairs)
    return list(out.values())


def on_device(coefficients, energy_gaps, metric_blocks, metric_index, coulomb_blocks, coulomb_index):
    c = coefficients.reshape(ROWS, BS, BS)
    s, v = metric_blocks, coulomb_blocks
    first_row = lax.axis_index("sec") * ROWS
    s_index, v_index = positions(metric_index, first_row), positions(coulomb_index, first_row)
    gaps = energy_gaps.reshape(1, BS)

    odd = lax.axis_index("sec") % 2 == 1
    c_far, c_near = halo(jnp.where(odd, c[56:], c[:8]), jnp.where(odd, c[:8], c[56:]))
    first, second, layer1, c_edge, s_edge, v_edge, v_mid, s_mid, s_out = inner(s_index, v_index, c, s, v)
    f_sends = edges(first_edges_kernel, s_index, c_far, c_near, c_edge, s_edge)
    f_halos = halo(*f_sends)
    e_low, e_high, *inside = middle(s_index, v_index, *f_sends, first, second, layer1, v_mid, s_mid)
    inside = spread_y(inside)
    e_sends = edges(second_edges_kernel, v_index, *f_halos, *f_sends, first, v_edge, e_low)
    e_halos = halo(*e_sends)
    layer3 = outer(s_index, *e_sends, e_low, e_high, second, s_out)
    outside = last(
        s_index, *e_halos, *e_sends, e_low, e_high, s_edge, gaps, layer3, *inside[1:]
    )
    outside = spread_y(outside)
    own, *others = product(*inside, *outside)
    sent = [swap(others[step * NZ + flip - 1], step, 0, flip) for step, flip in ((0, 1), (1, 0), (3, 0), (2, 0), (1, 1), (3, 1), (2, 1))]
    return add_up(own, sent)


def solution(mesh):
    placed = (
        P("sec", "grp"),
        P("grp"),
        P("sec", None, None, None),
        P("sec", None),
        P("sec", None, None, None),
        P("sec", None),
    )
    return jax.shard_map(
        on_device, mesh=mesh, in_specs=placed, out_specs=P("sec", "grp", None), check_vma=False
    )
```

```python
import jax
import jax.numpy as jnp
from jax import lax
from jax.experimental import pallas as pl
from jax.experimental.pallas import tpu as pltpu
from jax.sharding import PartitionSpec as P

BS = 128
ROWS = 64
REACH = 8
NBLK = 512
QC = 256
NX, NY, NZ = 4, 4, 2

frequency_sq = 1.0

VMEM = pl.BlockSpec(memory_space=pltpu.VMEM)
SMEM = pl.BlockSpec(memory_space=pltpu.SMEM)
HBM = pl.BlockSpec(memory_space=pltpu.HBM)
BF = jnp.bfloat16
F32 = jnp.float32


def blocks_of(count):
    return jax.ShapeDtypeStruct((count, BS, BS), BF)


def params(mib):
    return pltpu.CompilerParams(vmem_limit_bytes=mib * 2**20)


def cost(row_ops, nbytes):
    return pl.CostEstimate(
        flops=row_ops * 4 * BS**3, bytes_accessed=nbytes, transcendentals=0
    )


def coords():
    grp = lax.axis_index("grp")
    return grp // (NY * NZ), (grp // NZ) % NY, grp % NZ


def positions(index, first_row):
    rows = lax.broadcasted_iota(jnp.int32, (1, ROWS), 1)
    named = index.T[1:]
    distance = named - (first_row + rows)
    distance = jnp.where(distance >= NBLK // 2, distance - NBLK, distance)
    distance = jnp.where(distance < -(NBLK // 2), distance + NBLK, distance)
    return jnp.where(named >= 0, rows + distance, -NBLK)


def as_column(values):
    here = lax.broadcasted_iota(jnp.int32, (ROWS, ROWS), 0) == lax.broadcasted_iota(
        jnp.int32, (ROWS, ROWS), 1
    )
    column = jnp.sum(jnp.where(here, values, 0), axis=1, keepdims=True)
    return jnp.broadcast_to(column, (ROWS, BS))


def neighbour(index_ref, row):
    other = jnp.max(index_ref[pl.ds(row, 1), 0:1])
    live = other > -NBLK
    return jnp.where(live, other, row), live


def row_product(x, field_ref, base, row, index_ref):
    other, live = neighbour(index_ref, row)
    own = field_ref[row - base]
    far = jnp.where(live, field_ref[other - base], jnp.zeros((BS, BS), BF))
    return jnp.dot(
        jnp.concatenate([x[0], x[1]], axis=1),
        jnp.concatenate([own, far], axis=0),
        preferred_element_type=F32,
    ).astype(BF)


def rows_loop(first, count, body):
    def step(k, carry):
        body(first + k)
        return carry

    lax.fori_loop(0, count, step, 0, unroll=16)


def layer_start(layer, y):
    low, high = 8 * (4 - layer), 64 - 8 * (4 - layer) - 8
    if layer % 2 == 0:
        return jnp.where(y < 2, low + 4 * y, high + 4 * (y - 2))
    return jnp.where(y < 2, high + 4 * y, low + 4 * (y - 2))


def stored_slot(layer, start):
    low = 8 * (4 - layer)
    return jnp.where(start < 32, start - low, start + low - 48)


def inner_kernel(
    s_row, v_row, c_hbm, s_hbm, v_hbm,
    s_index, v_index, first, second, layer1, c_edge, s_edge, v_edge, v_mid, s_mid, s_out,
    c, s, v, sems,
):
    def load(k, source, target, at, to, count):
        return pltpu.make_async_copy(source.at[pl.ds(at, count)], target.at[pl.ds(to, count)], sems.at[k])

    copies = [
        load(0, c_hbm, c, 0, 0, 64),
        load(1, s_hbm, s, 8, 0, 16),
        load(2, s_hbm, s, 24, 16, 16),
        load(3, s_hbm, s, 40, 32, 16),
        load(4, v_hbm, v, 16, 0, 32),
        load(5, c_hbm, c_edge, 0, 0, 16),
        load(6, c_hbm, c_edge, 48, 16, 16),
    ]
    pieces = ((s_hbm, s_edge, 0), (v_hbm, v_edge, 0), (v_hbm, v_mid, 8), (s_hbm, s_mid, 16), (s_hbm, s_out, 8))
    for source, target, at in pieces:
        copies.append(load(len(copies), source, target, at, 0, 8))
        copies.append(load(len(copies), source, target, 56 - at, 8, 8))
    for copy in copies[:5]:
        copy.start()
    s_index[...] = as_column(s_row[...])
    v_index[...] = as_column(v_row[...])
    copies[0].wait()

    def one(row):
        first[row - 8] = row_product(s[row - 8], c, 0, row, s_index)

    for k in range(3):
        copies[1 + k].wait()
        rows_loop(8 + 16 * k, 16, one)
        if k == 0:
            for copy in copies[5:]:
                copy.start()
    copies[4].wait()

    def two(row):
        second[row - 16] = row_product(v[row - 16], first, 8, row, v_index)

    rows_loop(16, 32, two)
    _, y, _ = coords()
    for step in range(NY):
        start = layer_start(1, (y + step) % NY)
        for k in range(4):
            layer1[4 * step + k] = row_product(s[start + k - 8], second, 16, start + k, s_index)
    for copy in copies[5:]:
        copy.wait()


def inner(s_index, v_index, c, s, v):
    stored = jax.ShapeDtypeStruct((16, 2, BS, BS), BF)
    column = jax.ShapeDtypeStruct((ROWS, BS), jnp.int32)
    return pl.pallas_call(
        inner_kernel,
        out_shape=[column] * 2 + [blocks_of(48), blocks_of(32), blocks_of(16), blocks_of(32)] + [stored] * 5,
        in_specs=[VMEM, VMEM, HBM, HBM, HBM],
        out_specs=[VMEM] * 11,
        scratch_shapes=[
            pltpu.VMEM((64, BS, BS), BF),
            pltpu.VMEM((48, 2, BS, BS), BF),
            pltpu.VMEM((32, 2, BS, BS), BF),
            pltpu.SemaphoreType.DMA((17,)),
        ],
        compiler_params=params(44),
        cost_estimate=cost(96, 14 * 2**20),
    )(s_index, v_index, c, s, v)


def place(ref, far, near, head_at, tail_at):
    odd = lax.axis_index("sec") % 2
    ref[pl.ds(jnp.where(odd == 1, tail_at, head_at), 8)] = far[...]
    ref[pl.ds(jnp.where(odd == 1, head_at, tail_at), 8)] = near[...]


def edge_rows(index, ext, x, far, near):
    odd = lax.axis_index("sec") % 2
    for out, high in ((far, odd), (near, 1 - odd)):
        for k in range(8):
            out[k] = row_product(x[8 * high + k], ext, 32 * high - 8, 56 * high + k, index)


def first_edges_kernel(index, far_halo, near_halo, c, x, far, near, ext):
    place(ext, far_halo, near_halo, 0, 40)
    ext[8:40] = c[...]
    edge_rows(index, ext, x, far, near)


def second_edges_kernel(
    index, far_halo, near_halo, f_far, f_near, first, x, after, far, near, ext
):
    place(ext, far_halo, near_halo, 0, 40)
    place(ext, f_far, f_near, 8, 32)
    ext[16:24] = first[0:8]
    ext[24:32] = first[40:48]
    edge_rows(index, ext, x, far, near)


def edges(kernel, *operands):
    return pl.pallas_call(
        kernel,
        out_shape=[blocks_of(8)] * 2,
        in_specs=[VMEM] + [VMEM] * (len(operands) - 1),
        out_specs=[VMEM] * 2,
        scratch_shapes=[pltpu.VMEM((48, BS, BS), BF)],
        compiler_params=params(4),
        cost_estimate=cost(16, 3 * 2**20),
    )(*operands)


def middle_kernel(
    s_index, v_index, far, near, first, second, layer1, v, s, low_out, high_out, b0, b1, b2, b3, f, e
):
    place(f, far, near, 0, 40)
    f[8:24] = first[0:16]
    f[24:40] = first[32:48]
    for k in range(8):
        low_out[k] = row_product(v[k], f, 0, 8 + k, v_index)
        high_out[k] = row_product(v[8 + k], f, 16, 48 + k, v_index)
    e[0:8] = low_out[...]
    e[8:40] = second[...]
    e[40:48] = high_out[...]
    _, y, _ = coords()
    for step, out in enumerate((b0, b1, b2, b3)):
        out[0:4] = layer1[4 * step : 4 * step + 4]
        start = layer_start(2, (y + step) % NY)
        slot = stored_slot(2, start)
        for k in range(4):
            out[4 + k] = row_product(s[slot + k], e, 8, start + k, s_index)


def middle(*operands):
    return pl.pallas_call(
        middle_kernel,
        out_shape=[blocks_of(8)] * 6,
        in_specs=[VMEM, VMEM] + [VMEM] * 7,
        out_specs=[VMEM] * 6,
        scratch_shapes=[pltpu.VMEM((48, BS, BS), BF), pltpu.VMEM((48, BS, BS), BF)],
        compiler_params=params(4),
        cost_estimate=cost(32, 8 * 2**20),
    )(*operands)


def outer_kernel(index, far, near, low, high, second, s, layer3, e):
    place(e, far, near, 0, 40)
    e[8:16] = low[...]
    e[16:24] = second[0:8]
    e[24:32] = second[24:32]
    e[32:40] = high[...]
    _, y, _ = coords()
    for step in range(NY):
        start = layer_start(3, (y + step) % NY)
        slot = stored_slot(3, start)
        base = jnp.where(start < 32, 0, 16)
        for k in range(4):
            layer3[4 * step + k] = row_product(s[slot + k], e, base, start + k, index)


def outer(*operands):
    return pl.pallas_call(
        outer_kernel,
        out_shape=blocks_of(16),
        in_specs=[VMEM] + [VMEM] * 6,
        out_specs=VMEM,
        scratch_shapes=[pltpu.VMEM((48, BS, BS), BF)],
        compiler_params=params(4),
        cost_estimate=cost(16, 4 * 2**20),
    )(*operands)


def last_kernel(
    index, far_halo, near_halo, far, near, low, high, s, gaps, layer3, after1, after2, after3,
    b0, b1, b2, b3, e,
):
    place(e, far_halo, near_halo, 0, 40)
    place(e, far, near, 8, 32)
    e[16:24] = low[...]
    e[24:32] = high[...]
    gap = gaps[...]
    weight = 4.0 * gap / (gap * gap + frequency_sq)
    _, y, _ = coords()
    for k in range(2):
        value = row_product(s[k], e, -8, k, index)
        weighted = (value.astype(F32) * weight).astype(BF)
        for out in (b0, b1, b2, b3):
            out[8 + k] = weighted
    for step, out in enumerate((b0, b1, b2, b3)):
        out[0:4] = layer3[4 * step : 4 * step + 4]
        start = layer_start(4, (y + step) % NY)
        slot = stored_slot(4, start)
        base = jnp.where(start < 32, -8, 24)
        for k in range(4):
            out[4 + k] = row_product(s[slot + k], e, base, start + k, index)


def last(*operands):
    return pl.pallas_call(
        last_kernel,
        out_shape=[blocks_of(10)] * 4,
        in_specs=[VMEM] + [VMEM] * 12,
        out_specs=[VMEM] * 4,
        scratch_shapes=[pltpu.VMEM((48, BS, BS), BF)],
        compiler_params=params(4),
        cost_estimate=cost(18, 4 * 2**20),
    )(*operands)


def product_kernel(*refs):
    inside, outside = refs[:4], refs[4:8]
    own, outs, b, w = refs[8], refs[9:16], refs[16], refs[17]
    for source in range(4):
        lanes = slice(source * BS, (source + 1) * BS)
        for k in range(2):
            b[k, :, lanes] = inside[source][4 * k : 4 * k + 4].reshape(4 * BS, BS)
            b[2 + k, :, lanes] = outside[source][4 * k : 4 * k + 4].reshape(4 * BS, BS)
        w[:, lanes] = outside[source][8:10].reshape(QC, BS)
    x, y, z = coords()
    for step in range(NX):
        to = x ^ step
        near = jnp.where(to == 2, 0, jnp.where(to == 1, 1, jnp.where(to == 3, 2, 3)))
        away = jnp.where(to == 1, 0, jnp.where(to == 2, 1, jnp.where(to == 0, 2, 3)))
        layer = jnp.where(y < 2, near, away)
        for flip in range(NZ):
            half = z ^ flip
            tile = lax.dot_general(
                b[layer, pl.ds(pl.multiple_of(half * QC, QC), QC), :],
                w[...],
                (((1,), (1,)), ((), ())),
                preferred_element_type=F32,
            )
            if step == 0 and flip == 0:
                own[...] = tile
            else:
                outs[step * NZ + flip - 1][...] = tile.astype(BF)


def product(*operands):
    tile = jax.ShapeDtypeStruct((QC, QC), BF)
    return pl.pallas_call(
        product_kernel,
        out_shape=[jax.ShapeDtypeStruct((QC, QC), F32)] + [tile] * 7,
        in_specs=[VMEM] * 8,
        out_specs=[VMEM] * 8,
        scratch_shapes=[pltpu.VMEM((4, 4 * BS, 4 * BS), BF), pltpu.VMEM((QC, 4 * BS), BF)],
        compiler_params=params(8),
        cost_estimate=pl.CostEstimate(
            flops=2 * 2048 * 512 * 256, bytes_accessed=8 * 2**20, transcendentals=0
        ),
    )(*operands)


def add_kernel(*refs):
    total = refs[0][...]
    for ref in refs[1:8]:
        total += ref[...].astype(F32)
    refs[8][0] = total


def add_up(own, others):
    return pl.pallas_call(
        add_kernel,
        out_shape=jax.ShapeDtypeStruct((1, QC, QC), F32),
        in_specs=[VMEM] * 8,
        out_specs=VMEM,
        compiler_params=params(8),
        cost_estimate=pl.CostEstimate(flops=8 * QC * QC, bytes_accessed=2**20, transcendentals=0),
    )(own, *others)


def swap(value, dx, dy, dz):
    pairs = []
    for x in range(NX):
        for y in range(NY):
            for z in range(NZ):
                pairs.append(((x * NY + y) * NZ + z, ((x ^ dx) * NY + (y ^ dy)) * NZ + (z ^ dz)))
    return lax.ppermute(value, "grp", pairs)


def halo(far, near):
    count = lax.axis_size("sec")
    far_pairs = [(i, (i + 1 if i % 2 else i - 1) % count) for i in range(count)]
    near_pairs = [(i, i ^ 1) for i in range(count)]
    return lax.ppermute(far, "sec", far_pairs), lax.ppermute(near, "sec", near_pairs)


def spread_y(parts, order=(1, 3, 2)):
    out = {0: parts[0]}
    for d in order:
        pairs = []
        for k in range(NX * NY * NZ):
            x, y, z = k // (NY * NZ), k // NZ % NY, k % NZ
            pairs.append((k, (x * NY + (y + d) % NY) * NZ + z))
        out[d] = lax.ppermute(parts[d], "grp", pairs)
    return list(out.values())


def on_device(coefficients, energy_gaps, metric_blocks, metric_index, coulomb_blocks, coulomb_index):
    c = coefficients.reshape(ROWS, BS, BS)
    s, v = metric_blocks, coulomb_blocks
    first_row = lax.axis_index("sec") * ROWS
    s_row, v_row = positions(metric_index, first_row), positions(coulomb_index, first_row)
    gaps = energy_gaps.reshape(1, BS)

    odd = lax.axis_index("sec") % 2 == 1
    c_far, c_near = halo(jnp.where(odd, c[56:], c[:8]), jnp.where(odd, c[:8], c[56:]))
    s_index, v_index, first, second, layer1, *edges_of = inner(s_row, v_row, c, s, v)
    c_edge, s_edge, v_edge, v_mid, s_mid, s_out = edges_of
    f_sends = edges(first_edges_kernel, s_index, c_far, c_near, c_edge, s_edge)
    f_halos = halo(*f_sends)
    e_low, e_high, *inside = middle(s_index, v_index, *f_sends, first, second, layer1, v_mid, s_mid)
    inside = spread_y(inside)
    e_sends = edges(second_edges_kernel, v_index, *f_halos, *f_sends, first, v_edge, e_low)
    e_halos = halo(*e_sends)
    layer3 = outer(s_index, *e_sends, e_low, e_high, second, s_out)
    outside = last(
        s_index, *e_halos, *e_sends, e_low, e_high, s_edge, gaps, layer3, *inside[1:]
    )
    outside = spread_y(outside)
    own, *others = product(*inside, *outside)
    sent = [swap(others[step * NZ + flip - 1], step, 0, flip) for step, flip in ((0, 1), (1, 0), (3, 0), (2, 0), (1, 1), (3, 1), (2, 1))]
    return add_up(own, sent)


def solution(mesh):
    placed = (
        P("sec", "grp"),
        P("grp"),
        P("sec", None, None, None),
        P("sec", None),
        P("sec", None, None, None),
        P("sec", None),
    )
    return jax.shard_map(
        on_device, mesh=mesh, in_specs=placed, out_specs=P("sec", "grp", None), check_vma=False
    )
```

```python
import jax
import jax.numpy as jnp
from jax import lax
from jax.experimental import pallas as pl
from jax.experimental.pallas import tpu as pltpu
from jax.sharding import PartitionSpec as P

BS = 128
ROWS = 64
REACH = 8
NBLK = 512
QC = 256
NX, NY, NZ = 4, 4, 2

frequency_sq = 1.0

DIRECT = ((1, 0), (3, 0), (1, 1), (3, 1))

VMEM = pl.BlockSpec(memory_space=pltpu.VMEM)
SMEM = pl.BlockSpec(memory_space=pltpu.SMEM)
HBM = pl.BlockSpec(memory_space=pltpu.HBM)
BF = jnp.bfloat16
F32 = jnp.float32


def blocks_of(count):
    return jax.ShapeDtypeStruct((count, BS, BS), BF)


def params(mib):
    return pltpu.CompilerParams(vmem_limit_bytes=mib * 2**20)


def cost(row_ops, nbytes):
    return pl.CostEstimate(
        flops=row_ops * 4 * BS**3, bytes_accessed=nbytes, transcendentals=0
    )


def coords():
    grp = lax.axis_index("grp")
    return grp // (NY * NZ), (grp // NZ) % NY, grp % NZ


def positions(index, first_row):
    rows = lax.broadcasted_iota(jnp.int32, (1, ROWS), 1)
    named = index.T[1:]
    distance = named - (first_row + rows)
    distance = jnp.where(distance >= NBLK // 2, distance - NBLK, distance)
    distance = jnp.where(distance < -(NBLK // 2), distance + NBLK, distance)
    return jnp.where(named >= 0, rows + distance, -NBLK)


def as_column(values):
    here = lax.broadcasted_iota(jnp.int32, (ROWS, ROWS), 0) == lax.broadcasted_iota(
        jnp.int32, (ROWS, ROWS), 1
    )
    column = jnp.sum(jnp.where(here, values, 0), axis=1, keepdims=True)
    return jnp.broadcast_to(column, (ROWS, BS))


def neighbour(index_ref, row):
    other = jnp.max(index_ref[pl.ds(row, 1), 0:1])
    live = other > -NBLK
    return jnp.where(live, other, row), live


def row_product(x, field_ref, base, row, index_ref):
    other, live = neighbour(index_ref, row)
    own = field_ref[row - base]
    far = jnp.where(live, field_ref[other - base], jnp.zeros((BS, BS), BF))
    return jnp.dot(
        jnp.concatenate([x[0], x[1]], axis=1),
        jnp.concatenate([own, far], axis=0),
        preferred_element_type=F32,
    ).astype(BF)


def rows_loop(first, count, body):
    def step(k, carry):
        body(first + k)
        return carry

    lax.fori_loop(0, count, step, 0, unroll=16)


def layer_start(layer, y):
    low, high = 8 * (4 - layer), 64 - 8 * (4 - layer) - 8
    if layer % 2 == 0:
        return jnp.where(y < 2, low + 4 * y, high + 4 * (y - 2))
    return jnp.where(y < 2, high + 4 * y, low + 4 * (y - 2))


def stored_slot(layer, start):
    low = 8 * (4 - layer)
    return jnp.where(start < 32, start - low, start + low - 48)


def inner_kernel(
    s_row, v_row, c_hbm, s_hbm, v_hbm,
    s_index, v_index, first, second, layer1, c_edge, s_edge, v_edge, v_mid, s_mid, s_out,
    c, s, v, sems,
):
    def load(k, source, target, at, to, count):
        return pltpu.make_async_copy(source.at[pl.ds(at, count)], target.at[pl.ds(to, count)], sems.at[k])

    copies = [
        load(0, c_hbm, c, 0, 0, 64),
        load(1, s_hbm, s, 8, 0, 16),
        load(2, s_hbm, s, 24, 16, 16),
        load(3, s_hbm, s, 40, 32, 16),
        load(4, v_hbm, v, 16, 0, 32),
        load(5, c_hbm, c_edge, 0, 0, 16),
        load(6, c_hbm, c_edge, 48, 16, 16),
    ]
    pieces = ((s_hbm, s_edge, 0), (v_hbm, v_edge, 0), (v_hbm, v_mid, 8), (s_hbm, s_mid, 16), (s_hbm, s_out, 8))
    for source, target, at in pieces:
        copies.append(load(len(copies), source, target, at, 0, 8))
        copies.append(load(len(copies), source, target, 56 - at, 8, 8))
    for copy in copies[:5]:
        copy.start()
    s_index[...] = as_column(s_row[...])
    v_index[...] = as_column(v_row[...])
    copies[0].wait()

    def one(row):
        first[row - 8] = row_product(s[row - 8], c, 0, row, s_index)

    for k in range(3):
        copies[1 + k].wait()
        rows_loop(8 + 16 * k, 16, one)
        if k == 0:
            for copy in copies[5:]:
                copy.start()
    copies[4].wait()

    def two(row):
        second[row - 16] = row_product(v[row - 16], first, 8, row, v_index)

    rows_loop(16, 32, two)
    _, y, _ = coords()
    for step in range(NY):
        start = layer_start(1, (y + step) % NY)
        for k in range(4):
            layer1[4 * step + k] = row_product(s[start + k - 8], second, 16, start + k, s_index)
    for copy in copies[5:]:
        copy.wait()


def inner(s_index, v_index, c, s, v):
    stored = jax.ShapeDtypeStruct((16, 2, BS, BS), BF)
    column = jax.ShapeDtypeStruct((ROWS, BS), jnp.int32)
    return pl.pallas_call(
        inner_kernel,
        out_shape=[column] * 2 + [blocks_of(48), blocks_of(32), blocks_of(16), blocks_of(32)] + [stored] * 5,
        in_specs=[VMEM, VMEM, HBM, HBM, HBM],
        out_specs=[VMEM] * 11,
        scratch_shapes=[
            pltpu.VMEM((64, BS, BS), BF),
            pltpu.VMEM((48, 2, BS, BS), BF),
            pltpu.VMEM((32, 2, BS, BS), BF),
            pltpu.SemaphoreType.DMA((17,)),
        ],
        compiler_params=params(44),
        cost_estimate=cost(96, 14 * 2**20),
    )(s_index, v_index, c, s, v)


def place(ref, far, near, head_at, tail_at):
    odd = lax.axis_index("sec") % 2
    ref[pl.ds(jnp.where(odd == 1, tail_at, head_at), 8)] = far[...]
    ref[pl.ds(jnp.where(odd == 1, head_at, tail_at), 8)] = near[...]


def edge_rows(index, ext, x, far, near):
    odd = lax.axis_index("sec") % 2
    for out, high in ((far, odd), (near, 1 - odd)):
        for k in range(8):
            out[k] = row_product(x[8 * high + k], ext, 32 * high - 8, 56 * high + k, index)


def first_edges_kernel(index, far_halo, near_halo, c, x, far, near, ext):
    place(ext, far_halo, near_halo, 0, 40)
    ext[8:40] = c[...]
    edge_rows(index, ext, x, far, near)


def second_edges_kernel(
    index, far_halo, near_halo, f_far, f_near, first, x, after, far, near, ext
):
    place(ext, far_halo, near_halo, 0, 40)
    place(ext, f_far, f_near, 8, 32)
    ext[16:24] = first[0:8]
    ext[24:32] = first[40:48]
    edge_rows(index, ext, x, far, near)


def edges(kernel, *operands):
    return pl.pallas_call(
        kernel,
        out_shape=[blocks_of(8)] * 2,
        in_specs=[VMEM] + [VMEM] * (len(operands) - 1),
        out_specs=[VMEM] * 2,
        scratch_shapes=[pltpu.VMEM((48, BS, BS), BF)],
        compiler_params=params(4),
        cost_estimate=cost(16, 3 * 2**20),
    )(*operands)


def middle_kernel(
    s_index, v_index, far, near, first, second, layer1, v, s, low_out, high_out, b0, b1, b2, b3, f, e
):
    place(f, far, near, 0, 40)
    f[8:24] = first[0:16]
    f[24:40] = first[32:48]
    for k in range(8):
        low_out[k] = row_product(v[k], f, 0, 8 + k, v_index)
        high_out[k] = row_product(v[8 + k], f, 16, 48 + k, v_index)
    e[0:8] = low_out[...]
    e[8:40] = second[...]
    e[40:48] = high_out[...]
    _, y, _ = coords()
    for step, out in enumerate((b0, b1, b2, b3)):
        out[0:4] = layer1[4 * step : 4 * step + 4]
        start = layer_start(2, (y + step) % NY)
        slot = stored_slot(2, start)
        for k in range(4):
            out[4 + k] = row_product(s[slot + k], e, 8, start + k, s_index)


def middle(*operands):
    return pl.pallas_call(
        middle_kernel,
        out_shape=[blocks_of(8)] * 6,
        in_specs=[VMEM, VMEM] + [VMEM] * 7,
        out_specs=[VMEM] * 6,
        scratch_shapes=[pltpu.VMEM((48, BS, BS), BF), pltpu.VMEM((48, BS, BS), BF)],
        compiler_params=params(4),
        cost_estimate=cost(32, 8 * 2**20),
    )(*operands)


def outer_kernel(index, far, near, low, high, second, s, layer3, e):
    place(e, far, near, 0, 40)
    e[8:16] = low[...]
    e[16:24] = second[0:8]
    e[24:32] = second[24:32]
    e[32:40] = high[...]
    _, y, _ = coords()
    for step in range(NY):
        start = layer_start(3, (y + step) % NY)
        slot = stored_slot(3, start)
        base = jnp.where(start < 32, 0, 16)
        for k in range(4):
            layer3[4 * step + k] = row_product(s[slot + k], e, base, start + k, index)


def outer(*operands):
    return pl.pallas_call(
        outer_kernel,
        out_shape=blocks_of(16),
        in_specs=[VMEM] + [VMEM] * 6,
        out_specs=VMEM,
        scratch_shapes=[pltpu.VMEM((48, BS, BS), BF)],
        compiler_params=params(4),
        cost_estimate=cost(16, 4 * 2**20),
    )(*operands)


def last_kernel(
    index, far_halo, near_halo, far, near, low, high, s, gaps, layer3, after1, after2, after3,
    b0, b1, b2, b3, e,
):
    place(e, far_halo, near_halo, 0, 40)
    place(e, far, near, 8, 32)
    e[16:24] = low[...]
    e[24:32] = high[...]
    gap = gaps[...]
    weight = 4.0 * gap / (gap * gap + frequency_sq)
    _, y, _ = coords()
    for k in range(2):
        value = row_product(s[k], e, -8, k, index)
        weighted = (value.astype(F32) * weight).astype(BF)
        for out in (b0, b1, b2, b3):
            out[8 + k] = weighted
    for step, out in enumerate((b0, b1, b2, b3)):
        out[0:4] = layer3[4 * step : 4 * step + 4]
        start = layer_start(4, (y + step) % NY)
        slot = stored_slot(4, start)
        base = jnp.where(start < 32, -8, 24)
        for k in range(4):
            out[4 + k] = row_product(s[slot + k], e, base, start + k, index)


def last(*operands):
    return pl.pallas_call(
        last_kernel,
        out_shape=[blocks_of(10)] * 4,
        in_specs=[VMEM] + [VMEM] * 12,
        out_specs=[VMEM] * 4,
        scratch_shapes=[pltpu.VMEM((48, BS, BS), BF)],
        compiler_params=params(4),
        cost_estimate=cost(18, 4 * 2**20),
    )(*operands)


def chunk(inside, outside, to, half):
    _, y, _ = coords()
    near = jnp.where(to == 2, 0, jnp.where(to == 1, 1, jnp.where(to == 3, 2, 3)))
    away = jnp.where(to == 1, 0, jnp.where(to == 2, 1, jnp.where(to == 0, 2, 3)))
    layer = jnp.where(y < 2, near, away)
    rows = pl.ds(4 * (layer % 2) + 2 * half, 2)
    left = [
        jnp.where(layer < 2, inner_part[rows], outer_part[rows]).reshape(QC, BS)
        for inner_part, outer_part in zip(inside, outside)
    ]
    right = [part[8:10].reshape(QC, BS) for part in outside]
    return lax.dot_general(
        jnp.concatenate(left, axis=1),
        jnp.concatenate(right, axis=1),
        (((1,), (1,)), ((), ())),
        preferred_element_type=F32,
    )


def across_kernel(*refs):
    inside, outside, out = refs[:4], refs[4:8], refs[8]
    x, _, z = coords()
    out[0] = chunk(inside, outside, x, z ^ 1).astype(BF)
    out[1] = chunk(inside, outside, x ^ 2, z ^ 1).astype(BF)


def product_kernel(*refs):
    inside, outside = refs[:4], refs[4:8]
    own, passed, outs = refs[9], refs[10], refs[11:]
    x, _, z = coords()
    for out, (step, flip) in zip(outs, DIRECT):
        out[...] = chunk(inside, outside, x ^ step, z ^ flip).astype(BF)
    passed[...] = chunk(inside, outside, x ^ 2, z)
    own[...] = chunk(inside, outside, x, z)


def product(kernel, tiles, out_shape, *operands):
    return pl.pallas_call(
        kernel,
        out_shape=out_shape,
        in_specs=[VMEM] * len(operands),
        out_specs=jax.tree.map(lambda _: VMEM, out_shape),
        compiler_params=params(8),
        cost_estimate=pl.CostEstimate(
            flops=2 * tiles * QC * QC * 512, bytes_accessed=2**20 * tiles, transcendentals=0
        ),
    )(*operands)


def pass_kernel(passed, arrived, out):
    out[...] = (passed[...] + arrived[1].astype(F32)).astype(BF)


def pass_on(passed, arrived):
    return pl.pallas_call(
        pass_kernel,
        out_shape=jax.ShapeDtypeStruct((QC, QC), BF),
        in_specs=[VMEM] * 2,
        out_specs=VMEM,
        compiler_params=params(4),
        cost_estimate=pl.CostEstimate(flops=QC * QC, bytes_accessed=2**19, transcendentals=0),
    )(passed, arrived)


def add_kernel(own, arrived, *refs):
    total = own[...] + arrived[0].astype(F32)
    for ref in refs[:-1]:
        total += ref[...].astype(F32)
    refs[-1][0] = total


def add_up(*operands):
    return pl.pallas_call(
        add_kernel,
        out_shape=jax.ShapeDtypeStruct((1, QC, QC), F32),
        in_specs=[VMEM] * len(operands),
        out_specs=VMEM,
        compiler_params=params(4),
        cost_estimate=pl.CostEstimate(flops=8 * QC * QC, bytes_accessed=2**20, transcendentals=0),
    )(*operands)


def swap(value, dx, dy, dz):
    pairs = []
    for x in range(NX):
        for y in range(NY):
            for z in range(NZ):
                pairs.append(((x * NY + y) * NZ + z, ((x ^ dx) * NY + (y ^ dy)) * NZ + (z ^ dz)))
    return lax.ppermute(value, "grp", pairs)


def halo(far, near):
    count = lax.axis_size("sec")
    far_pairs = [(i, (i + 1 if i % 2 else i - 1) % count) for i in range(count)]
    near_pairs = [(i, i ^ 1) for i in range(count)]
    return lax.ppermute(far, "sec", far_pairs), lax.ppermute(near, "sec", near_pairs)


def spread_y(parts, order=(1, 3, 2)):
    out = {0: parts[0]}
    for d in order:
        pairs = []
        for k in range(NX * NY * NZ):
            x, y, z = k // (NY * NZ), k // NZ % NY, k % NZ
            pairs.append((k, (x * NY + (y + d) % NY) * NZ + z))
        out[d] = lax.ppermute(parts[d], "grp", pairs)
    return list(out.values())


def on_device(coefficients, energy_gaps, metric_blocks, metric_index, coulomb_blocks, coulomb_index):
    c = coefficients.reshape(ROWS, BS, BS)
    s, v = metric_blocks, coulomb_blocks
    first_row = lax.axis_index("sec") * ROWS
    s_row, v_row = positions(metric_index, first_row), positions(coulomb_index, first_row)
    gaps = energy_gaps.reshape(1, BS)

    odd = lax.axis_index("sec") % 2 == 1
    c_far, c_near = halo(jnp.where(odd, c[56:], c[:8]), jnp.where(odd, c[:8], c[56:]))
    s_index, v_index, first, second, layer1, *edges_of = inner(s_row, v_row, c, s, v)
    c_edge, s_edge, v_edge, v_mid, s_mid, s_out = edges_of
    f_sends = edges(first_edges_kernel, s_index, c_far, c_near, c_edge, s_edge)
    f_halos = halo(*f_sends)
    e_low, e_high, *inside = middle(s_index, v_index, *f_sends, first, second, layer1, v_mid, s_mid)
    inside = spread_y(inside)
    e_sends = edges(second_edges_kernel, v_index, *f_halos, *f_sends, first, v_edge, e_low)
    e_halos = halo(*e_sends)
    layer3 = outer(s_index, *e_sends, e_low, e_high, second, s_out)
    outside = last(
        s_index, *e_halos, *e_sends, e_low, e_high, s_edge, gaps, layer3, *inside[1:]
    )
    outside = spread_y(outside)
    tile = jax.ShapeDtypeStruct((QC, QC), BF)
    whole = jax.ShapeDtypeStruct((QC, QC), F32)
    across = product(across_kernel, 2, jax.ShapeDtypeStruct((2, QC, QC), BF), *inside, *outside)
    arrived = swap(across, 0, 0, 1)
    own, passed, *direct = product(
        product_kernel, 6, [whole] * 2 + [tile] * len(DIRECT), *inside, *outside, across
    )
    direct = [swap(part, step, 0, flip) for part, (step, flip) in zip(direct, DIRECT)]
    last_tile = swap(pass_on(passed, arrived), 2, 0, 0)
    return add_up(own, arrived, *direct, last_tile)


def solution(mesh):
    placed = (
        P("sec", "grp"),
        P("grp"),
        P("sec", None, None, None),
        P("sec", None),
        P("sec", None, None, None),
        P("sec", None),
    )
    return jax.shard_map(
        on_device, mesh=mesh, in_specs=placed, out_specs=P("sec", "grp", None), check_vma=False
    )
```

```python
import functools

import jax
import jax.numpy as jnp
from jax import lax
from jax.experimental import pallas as pl
from jax.experimental.pallas import tpu as pltpu
from jax.sharding import PartitionSpec as P

BS = 128
ROWS = 64
REACH = 8
NBLK = 512
QC = 256
NX, NY, NZ = 4, 4, 2

frequency_sq = 1.0

DIRECT = ((1, 0), (3, 0), (1, 1), (3, 1))

VMEM = pl.BlockSpec(memory_space=pltpu.VMEM)
SMEM = pl.BlockSpec(memory_space=pltpu.SMEM)
HBM = pl.BlockSpec(memory_space=pltpu.HBM)
BF = jnp.bfloat16
F32 = jnp.float32


def blocks_of(count):
    return jax.ShapeDtypeStruct((count, BS, BS), BF)


def params(mib):
    return pltpu.CompilerParams(vmem_limit_bytes=mib * 2**20)


def cost(row_ops, nbytes):
    return pl.CostEstimate(
        flops=row_ops * 4 * BS**3, bytes_accessed=nbytes, transcendentals=0
    )


def coords():
    grp = lax.axis_index("grp")
    return grp // (NY * NZ), (grp // NZ) % NY, grp % NZ


def positions(index, first_row):
    rows = lax.broadcasted_iota(jnp.int32, (1, ROWS), 1)
    named = index.T[1:]
    distance = named - (first_row + rows)
    distance = jnp.where(distance >= NBLK // 2, distance - NBLK, distance)
    distance = jnp.where(distance < -(NBLK // 2), distance + NBLK, distance)
    return jnp.where(named >= 0, rows + distance, -NBLK)


def as_column(values):
    here = lax.broadcasted_iota(jnp.int32, (ROWS, ROWS), 0) == lax.broadcasted_iota(
        jnp.int32, (ROWS, ROWS), 1
    )
    column = jnp.sum(jnp.where(here, values, 0), axis=1, keepdims=True)
    return jnp.broadcast_to(column, (ROWS, BS))


def neighbour(index_ref, row):
    other = jnp.max(index_ref[pl.ds(row, 1), 0:1])
    live = other > -NBLK
    return jnp.where(live, other, row), live


def row_product(x, field_ref, base, row, index_ref):
    other, live = neighbour(index_ref, row)
    own = field_ref[row - base]
    far = jnp.where(live, field_ref[other - base], jnp.zeros((BS, BS), BF))
    return jnp.dot(
        jnp.concatenate([x[0], x[1]], axis=1),
        jnp.concatenate([own, far], axis=0),
        preferred_element_type=F32,
    ).astype(BF)


def rows_loop(first, count, body):
    def step(k, carry):
        body(first + k)
        return carry

    lax.fori_loop(0, count, step, 0, unroll=16)


def layer_start(layer, y):
    low, high = 8 * (4 - layer), 64 - 8 * (4 - layer) - 8
    if layer % 2 == 0:
        return jnp.where(y < 2, low + 4 * y, high + 4 * (y - 2))
    return jnp.where(y < 2, high + 4 * y, low + 4 * (y - 2))


def stored_slot(layer, start):
    low = 8 * (4 - layer)
    return jnp.where(start < 32, start - low, start + low - 48)


def inner_kernel(
    s_row, v_row, c_hbm, s_hbm, v_hbm,
    s_index, v_index, first, second, layer1, c_edge, s_edge, v_edge, v_mid, s_mid, s_out,
    c, s, v, sems,
):
    def load(k, source, target, at, to, count):
        return pltpu.make_async_copy(source.at[pl.ds(at, count)], target.at[pl.ds(to, count)], sems.at[k])

    copies = [
        load(0, c_hbm, c, 0, 0, 64),
        load(1, s_hbm, s, 8, 0, 16),
        load(2, s_hbm, s, 24, 16, 16),
        load(3, s_hbm, s, 40, 32, 16),
        load(4, v_hbm, v, 16, 0, 32),
        load(5, c_hbm, c_edge, 0, 0, 16),
        load(6, c_hbm, c_edge, 48, 16, 16),
    ]
    pieces = ((s_hbm, s_edge, 0), (v_hbm, v_edge, 0), (v_hbm, v_mid, 8), (s_hbm, s_mid, 16), (s_hbm, s_out, 8))
    for source, target, at in pieces:
        copies.append(load(len(copies), source, target, at, 0, 8))
        copies.append(load(len(copies), source, target, 56 - at, 8, 8))
    for copy in copies[:5]:
        copy.start()
    s_index[...] = as_column(s_row[...])
    v_index[...] = as_column(v_row[...])
    copies[0].wait()

    def one(row):
        first[row - 8] = row_product(s[row - 8], c, 0, row, s_index)

    for k in range(3):
        copies[1 + k].wait()
        rows_loop(8 + 16 * k, 16, one)
        if k == 0:
            for copy in copies[5:]:
                copy.start()
    copies[4].wait()

    def two(row):
        second[row - 16] = row_product(v[row - 16], first, 8, row, v_index)

    rows_loop(16, 32, two)
    _, y, _ = coords()
    for step in range(NY):
        start = layer_start(1, (y + step) % NY)
        for k in range(4):
            layer1[4 * step + k] = row_product(s[start + k - 8], second, 16, start + k, s_index)
    for copy in copies[5:]:
        copy.wait()


def inner(s_index, v_index, c, s, v):
    stored = jax.ShapeDtypeStruct((16, 2, BS, BS), BF)
    column = jax.ShapeDtypeStruct((ROWS, BS), jnp.int32)
    return pl.pallas_call(
        inner_kernel,
        out_shape=[column] * 2 + [blocks_of(48), blocks_of(32), blocks_of(16), blocks_of(32)] + [stored] * 5,
        in_specs=[VMEM, VMEM, HBM, HBM, HBM],
        out_specs=[VMEM] * 11,
        scratch_shapes=[
            pltpu.VMEM((64, BS, BS), BF),
            pltpu.VMEM((48, 2, BS, BS), BF),
            pltpu.VMEM((32, 2, BS, BS), BF),
            pltpu.SemaphoreType.DMA((17,)),
        ],
        compiler_params=params(44),
        cost_estimate=cost(96, 14 * 2**20),
    )(s_index, v_index, c, s, v)


def place(ref, far, near, head_at, tail_at):
    odd = lax.axis_index("sec") % 2
    ref[pl.ds(jnp.where(odd == 1, tail_at, head_at), 8)] = far[...]
    ref[pl.ds(jnp.where(odd == 1, head_at, tail_at), 8)] = near[...]


def edge_side(far):
    odd = lax.axis_index("sec") % 2
    return odd if far else 1 - odd


def edge_rows(index, ext, x, high, emit):
    for k in range(8):
        emit(k, row_product(x[8 * high + k], ext, 56 * high - 8, 56 * high + k, index))


def first_edge_kernel(far, index, halo, c, x, after, out, ext):
    high = edge_side(far)
    ext[pl.ds(16 * high, 8)] = halo[...]
    ext[pl.ds(8 - 8 * high, 16)] = c[pl.ds(16 * high, 16)]

    def emit(k, value):
        out[k] = value

    edge_rows(index, ext, x, high, emit)


def fill_ext(ext, high, halo, edge, inside, inside_at):
    ext[pl.ds(16 * high, 8)] = halo[...]
    ext[8:16] = edge[...]
    ext[pl.ds(16 - 16 * high, 8)] = inside[pl.ds(inside_at * high, 8)]


def second_edge_kernel(far, index, halo, edge, first, x, after, out, ext):
    high = edge_side(far)
    fill_ext(ext, high, halo, edge, first, 40)

    def emit(k, value):
        out[k] = value

    edge_rows(index, ext, x, high, emit)


def near_kernel(index, halo, edge, mid, x, out, ext):
    high = edge_side(False)
    fill_ext(ext, high, halo, edge, mid, 8)

    def emit(k, value):
        out[k] = value

    edge_rows(index, ext, x, high, emit)


def edge(kernel, *operands):
    return pl.pallas_call(
        kernel,
        out_shape=blocks_of(8),
        in_specs=[VMEM] + [VMEM] * (len(operands) - 1),
        out_specs=VMEM,
        scratch_shapes=[pltpu.VMEM((24, BS, BS), BF)],
        compiler_params=params(4),
        cost_estimate=cost(8, 2 * 2**20),
    )(*operands)


def middle_kernel(
    s_index, v_index, far, near, first, second, layer1, v, s, mid, b0, b1, b2, b3, f, e
):
    place(f, far, near, 0, 40)
    f[8:24] = first[0:16]
    f[24:40] = first[32:48]
    for k in range(8):
        mid[k] = row_product(v[k], f, 0, 8 + k, v_index)
        mid[8 + k] = row_product(v[8 + k], f, 16, 48 + k, v_index)
    e[0:8] = mid[0:8]
    e[8:40] = second[...]
    e[40:48] = mid[8:16]
    _, y, _ = coords()
    for step, out in enumerate((b0, b1, b2, b3)):
        out[0:4] = layer1[4 * step : 4 * step + 4]
        start = layer_start(2, (y + step) % NY)
        slot = stored_slot(2, start)
        for k in range(4):
            out[4 + k] = row_product(s[slot + k], e, 8, start + k, s_index)


def middle(*operands):
    return pl.pallas_call(
        middle_kernel,
        out_shape=[blocks_of(16)] + [blocks_of(8)] * 4,
        in_specs=[VMEM, VMEM] + [VMEM] * 7,
        out_specs=[VMEM] * 5,
        scratch_shapes=[pltpu.VMEM((48, BS, BS), BF), pltpu.VMEM((48, BS, BS), BF)],
        compiler_params=params(4),
        cost_estimate=cost(32, 8 * 2**20),
    )(*operands)


def outer_kernel(index, far, near, mid, second, s, layer3, e):
    place(e, far, near, 0, 40)
    e[8:16] = mid[0:8]
    e[16:24] = second[0:8]
    e[24:32] = second[24:32]
    e[32:40] = mid[8:16]
    _, y, _ = coords()
    for step in range(NY):
        start = layer_start(3, (y + step) % NY)
        slot = stored_slot(3, start)
        base = jnp.where(start < 32, 0, 16)
        for k in range(4):
            layer3[4 * step + k] = row_product(s[slot + k], e, base, start + k, index)


def outer(*operands):
    return pl.pallas_call(
        outer_kernel,
        out_shape=blocks_of(16),
        in_specs=[VMEM] + [VMEM] * 5,
        out_specs=VMEM,
        scratch_shapes=[pltpu.VMEM((48, BS, BS), BF)],
        compiler_params=params(4),
        cost_estimate=cost(16, 4 * 2**20),
    )(*operands)


def last_kernel(
    index, halo, edge, mid, x, near_rows, gaps, layer3, after1, after2, after3, b0, b1, b2, b3, ext, rows
):
    high = edge_side(True)
    rows[pl.ds(8 - 8 * high, 8)] = near_rows[...]
    fill_ext(ext, high, halo, edge, mid, 8)

    def emit(k, value):
        rows[8 * high + k] = value

    edge_rows(index, ext, x, high, emit)
    gap = gaps[...]
    weight = 4.0 * gap / (gap * gap + frequency_sq)
    weighted = (rows[0:2].astype(F32) * weight[None]).astype(BF)
    _, y, _ = coords()
    for step, out in enumerate((b0, b1, b2, b3)):
        out[0:4] = layer3[4 * step : 4 * step + 4]
        out[4:8] = rows[pl.ds(4 * ((y + step) % NY), 4)]
        out[8:10] = weighted


def last(*operands):
    return pl.pallas_call(
        last_kernel,
        out_shape=[blocks_of(10)] * 4,
        in_specs=[VMEM] + [VMEM] * 10,
        out_specs=[VMEM] * 4,
        scratch_shapes=[pltpu.VMEM((24, BS, BS), BF), pltpu.VMEM((16, BS, BS), BF)],
        compiler_params=params(4),
        cost_estimate=cost(8, 4 * 2**20),
    )(*operands)


def chunk(inside, outside, to, half):
    _, y, _ = coords()
    near = jnp.where(to == 2, 0, jnp.where(to == 1, 1, jnp.where(to == 3, 2, 3)))
    away = jnp.where(to == 1, 0, jnp.where(to == 2, 1, jnp.where(to == 0, 2, 3)))
    layer = jnp.where(y < 2, near, away)
    rows = pl.ds(4 * (layer % 2) + 2 * half, 2)
    left = [
        jnp.where(layer < 2, inner_part[rows], outer_part[rows]).reshape(QC, BS)
        for inner_part, outer_part in zip(inside, outside)
    ]
    right = [part[8:10].reshape(QC, BS) for part in outside]
    return lax.dot_general(
        jnp.concatenate(left, axis=1),
        jnp.concatenate(right, axis=1),
        (((1,), (1,)), ((), ())),
        preferred_element_type=F32,
    )


def across_kernel(*refs):
    inside, outside, out = refs[:4], refs[4:8], refs[8]
    x, _, z = coords()
    out[0] = chunk(inside, outside, x, z ^ 1).astype(BF)
    out[1] = chunk(inside, outside, x ^ 2, z ^ 1).astype(BF)


def product_kernel(*refs):
    inside, outside = refs[:4], refs[4:8]
    own, passed, outs = refs[9], refs[10], refs[11:]
    x, _, z = coords()
    for out, (step, flip) in zip(outs, DIRECT):
        out[...] = chunk(inside, outside, (x + step) % NX, z ^ flip).astype(BF)
    passed[...] = chunk(inside, outside, x ^ 2, z)
    own[...] = chunk(inside, outside, x, z)


def product(kernel, tiles, out_shape, *operands):
    return pl.pallas_call(
        kernel,
        out_shape=out_shape,
        in_specs=[VMEM] * len(operands),
        out_specs=jax.tree.map(lambda _: VMEM, out_shape),
        compiler_params=params(8),
        cost_estimate=pl.CostEstimate(
            flops=2 * tiles * QC * QC * 512, bytes_accessed=2**20 * tiles, transcendentals=0
        ),
    )(*operands)


def pass_kernel(passed, arrived, out):
    out[...] = (passed[...] + arrived[1].astype(F32)).astype(BF)


def pass_on(passed, arrived):
    return pl.pallas_call(
        pass_kernel,
        out_shape=jax.ShapeDtypeStruct((QC, QC), BF),
        in_specs=[VMEM] * 2,
        out_specs=VMEM,
        compiler_params=params(4),
        cost_estimate=pl.CostEstimate(flops=QC * QC, bytes_accessed=2**19, transcendentals=0),
    )(passed, arrived)


def add_kernel(own, arrived, *refs):
    total = own[...] + arrived[0].astype(F32)
    for ref in refs[:-1]:
        total += ref[...].astype(F32)
    refs[-1][0] = total


def add_up(*operands):
    return pl.pallas_call(
        add_kernel,
        out_shape=jax.ShapeDtypeStruct((1, QC, QC), F32),
        in_specs=[VMEM] * len(operands),
        out_specs=VMEM,
        compiler_params=params(4),
        cost_estimate=pl.CostEstimate(flops=8 * QC * QC, bytes_accessed=2**20, transcendentals=0),
    )(*operands)


def shift(value, dx, dy, dz):
    pairs = []
    for x in range(NX):
        for y in range(NY):
            for z in range(NZ):
                pairs.append(((x * NY + y) * NZ + z, ((x + dx) % NX * NY + (y ^ dy)) * NZ + (z ^ dz)))
    return lax.ppermute(value, "grp", pairs)


def halo(far, near):
    count = lax.axis_size("sec")
    far_pairs = [(i, (i + 1 if i % 2 else i - 1) % count) for i in range(count)]
    near_pairs = [(i, i ^ 1) for i in range(count)]
    return lax.ppermute(far, "sec", far_pairs), lax.ppermute(near, "sec", near_pairs)


def spread_y(parts, order=(1, 3, 2)):
    out = {0: parts[0]}
    for d in order:
        pairs = []
        for k in range(NX * NY * NZ):
            x, y, z = k // (NY * NZ), k // NZ % NY, k % NZ
            pairs.append((k, (x * NY + (y + d) % NY) * NZ + z))
        out[d] = lax.ppermute(parts[d], "grp", pairs)
    return list(out.values())


def on_device(coefficients, energy_gaps, metric_blocks, metric_index, coulomb_blocks, coulomb_index):
    c = coefficients.reshape(ROWS, BS, BS)
    s, v = metric_blocks, coulomb_blocks
    first_row = lax.axis_index("sec") * ROWS
    s_row, v_row = positions(metric_index, first_row), positions(coulomb_index, first_row)
    gaps = energy_gaps.reshape(1, BS)

    odd = lax.axis_index("sec") % 2 == 1
    c_far, c_near = halo(jnp.where(odd, c[56:], c[:8]), jnp.where(odd, c[:8], c[56:]))
    s_index, v_index, first, second, layer1, *edges_of = inner(s_row, v_row, c, s, v)
    c_edge, s_edge, v_edge, v_mid, s_mid, s_out = edges_of
    first_far, first_near = (functools.partial(first_edge_kernel, far) for far in (True, False))
    second_far, second_near = (functools.partial(second_edge_kernel, far) for far in (True, False))
    f_near = edge(first_near, s_index, c_near, c_edge, s_edge, layer1)
    f_far = edge(first_far, s_index, c_far, c_edge, s_edge, f_near)
    f_far_halo, f_near_halo = halo(f_far, f_near)
    mid, *inside = middle(s_index, v_index, f_far, f_near, first, second, layer1, v_mid, s_mid)
    inside = spread_y(inside)
    e_near = edge(second_near, v_index, f_near_halo, f_near, first, v_edge, mid)
    e_far = edge(second_far, v_index, f_far_halo, f_far, first, v_edge, e_near)
    e_far_halo, e_near_halo = halo(e_far, e_near)
    layer3 = outer(s_index, e_far, e_near, mid, second, s_out)
    b_near = edge(near_kernel, s_index, e_near_halo, e_near, mid, s_edge)
    outside = last(
        s_index, e_far_halo, e_far, mid, s_edge, b_near, gaps, layer3, *inside[1:]
    )
    outside = spread_y(outside)
    tile = jax.ShapeDtypeStruct((QC, QC), BF)
    whole = jax.ShapeDtypeStruct((QC, QC), F32)
    across = product(across_kernel, 2, jax.ShapeDtypeStruct((2, QC, QC), BF), *inside, *outside)
    arrived = shift(across, 0, 0, 1)
    own, passed, *direct = product(
        product_kernel, 6, [whole] * 2 + [tile] * len(DIRECT), *inside, *outside, across
    )
    direct = [shift(part, step, 0, flip) for part, (step, flip) in zip(direct, DIRECT)]
    last_tile = shift(pass_on(passed, arrived), 2, 0, 0)
    return add_up(own, arrived, *direct, last_tile)


def solution(mesh):
    placed = (
        P("sec", "grp"),
        P("grp"),
        P("sec", None, None, None),
        P("sec", None),
        P("sec", None, None, None),
        P("sec", None),
    )
    return jax.shard_map(
        on_device, mesh=mesh, in_specs=placed, out_specs=P("sec", "grp", None), check_vma=False
    )
```

```python
import functools

import jax
import jax.numpy as jnp
from jax import lax
from jax.experimental import pallas as pl
from jax.experimental.pallas import tpu as pltpu
from jax.sharding import PartitionSpec as P

BS = 128
ROWS = 64
REACH = 8
NBLK = 512
QC = 256
NX, NY, NZ = 4, 4, 2

frequency_sq = 1.0

DIRECT = ((1, 0), (3, 0), (3, 1), (1, 1))

VMEM = pl.BlockSpec(memory_space=pltpu.VMEM)
SMEM = pl.BlockSpec(memory_space=pltpu.SMEM)
HBM = pl.BlockSpec(memory_space=pltpu.HBM)
BF = jnp.bfloat16
F32 = jnp.float32


def blocks_of(count):
    return jax.ShapeDtypeStruct((count, BS, BS), BF)


def params(mib):
    return pltpu.CompilerParams(vmem_limit_bytes=mib * 2**20)


def cost(row_ops, nbytes):
    return pl.CostEstimate(
        flops=row_ops * 4 * BS**3, bytes_accessed=nbytes, transcendentals=0
    )


def coords():
    grp = lax.axis_index("grp")
    return grp // (NY * NZ), (grp // NZ) % NY, grp % NZ


def positions(index, first_row):
    rows = lax.broadcasted_iota(jnp.int32, (1, ROWS), 1)
    named = index.T[1:]
    distance = named - (first_row + rows)
    distance = jnp.where(distance >= NBLK // 2, distance - NBLK, distance)
    distance = jnp.where(distance < -(NBLK // 2), distance + NBLK, distance)
    return jnp.where(named >= 0, rows + distance, -NBLK)


def as_column(values):
    here = lax.broadcasted_iota(jnp.int32, (ROWS, ROWS), 0) == lax.broadcasted_iota(
        jnp.int32, (ROWS, ROWS), 1
    )
    column = jnp.sum(jnp.where(here, values, 0), axis=1, keepdims=True)
    return jnp.broadcast_to(column, (ROWS, BS))


def neighbour(index_ref, row):
    other = jnp.max(index_ref[pl.ds(row, 1), 0:1])
    live = other > -NBLK
    return jnp.where(live, other, row), live


def row_product(x, field_ref, base, row, index_ref):
    other, live = neighbour(index_ref, row)
    own = field_ref[row - base]
    far = jnp.where(live, field_ref[other - base], jnp.zeros((BS, BS), BF))
    return jnp.dot(
        jnp.concatenate([x[0], x[1]], axis=1),
        jnp.concatenate([own, far], axis=0),
        preferred_element_type=F32,
    ).astype(BF)


def rows_loop(first, count, body):
    def step(k, carry):
        body(first + k)
        return carry

    lax.fori_loop(0, count, step, 0, unroll=16)


def layer_start(layer, y):
    low, high = 8 * (4 - layer), 64 - 8 * (4 - layer) - 8
    if layer % 2 == 0:
        return jnp.where(y < 2, low + 4 * y, high + 4 * (y - 2))
    return jnp.where(y < 2, high + 4 * y, low + 4 * (y - 2))


def stored_slot(layer, start):
    low = 8 * (4 - layer)
    return jnp.where(start < 32, start - low, start + low - 48)


def inner_kernel(
    s_row, v_row, c_hbm, s_hbm, v_hbm,
    s_index, v_index, first, second, layer1, c_edge, s_edge, v_edge, v_mid, s_mid, s_out,
    c, s, v, sems,
):
    def load(k, source, target, at, to, count):
        return pltpu.make_async_copy(source.at[pl.ds(at, count)], target.at[pl.ds(to, count)], sems.at[k])

    copies = [
        load(0, c_hbm, c, 0, 0, 64),
        load(1, s_hbm, s, 8, 0, 16),
        load(2, s_hbm, s, 24, 16, 16),
        load(3, s_hbm, s, 40, 32, 16),
        load(4, v_hbm, v, 16, 0, 32),
        load(5, c_hbm, c_edge, 0, 0, 16),
        load(6, c_hbm, c_edge, 48, 16, 16),
    ]
    pieces = ((s_hbm, s_edge, 0), (v_hbm, v_edge, 0), (v_hbm, v_mid, 8), (s_hbm, s_mid, 16), (s_hbm, s_out, 8))
    for source, target, at in pieces:
        copies.append(load(len(copies), source, target, at, 0, 8))
        copies.append(load(len(copies), source, target, 56 - at, 8, 8))
    for copy in copies[:5]:
        copy.start()
    s_index[...] = as_column(s_row[...])
    v_index[...] = as_column(v_row[...])
    copies[0].wait()

    def one(row):
        first[row - 8] = row_product(s[row - 8], c, 0, row, s_index)

    for k in range(3):
        copies[1 + k].wait()
        rows_loop(8 + 16 * k, 16, one)
        if k == 0:
            for copy in copies[5:]:
                copy.start()
    copies[4].wait()

    def two(row):
        second[row - 16] = row_product(v[row - 16], first, 8, row, v_index)

    rows_loop(16, 32, two)
    _, y, _ = coords()
    for step in range(NY):
        start = layer_start(1, (y + step) % NY)
        for k in range(4):
            layer1[4 * step + k] = row_product(s[start + k - 8], second, 16, start + k, s_index)
    for copy in copies[5:]:
        copy.wait()


def inner(s_index, v_index, c, s, v):
    stored = jax.ShapeDtypeStruct((16, 2, BS, BS), BF)
    column = jax.ShapeDtypeStruct((ROWS, BS), jnp.int32)
    return pl.pallas_call(
        inner_kernel,
        out_shape=[column] * 2 + [blocks_of(48), blocks_of(32), blocks_of(16), blocks_of(32)] + [stored] * 5,
        in_specs=[VMEM, VMEM, HBM, HBM, HBM],
        out_specs=[VMEM] * 11,
        scratch_shapes=[
            pltpu.VMEM((64, BS, BS), BF),
            pltpu.VMEM((48, 2, BS, BS), BF),
            pltpu.VMEM((32, 2, BS, BS), BF),
            pltpu.SemaphoreType.DMA((17,)),
        ],
        compiler_params=params(44),
        cost_estimate=cost(96, 14 * 2**20),
    )(s_index, v_index, c, s, v)


def place(ref, far, near, head_at, tail_at):
    odd = lax.axis_index("sec") % 2
    ref[pl.ds(jnp.where(odd == 1, tail_at, head_at), 8)] = far[...]
    ref[pl.ds(jnp.where(odd == 1, head_at, tail_at), 8)] = near[...]


def edge_side(far):
    odd = lax.axis_index("sec") % 2
    return odd if far else 1 - odd


def edge_rows(index, ext, x, high, emit):
    for k in range(8):
        emit(k, row_product(x[8 * high + k], ext, 56 * high - 8, 56 * high + k, index))


def first_edge_kernel(far, index, halo, c, x, after, out, ext):
    high = edge_side(far)
    ext[pl.ds(16 * high, 8)] = halo[...]
    ext[pl.ds(8 - 8 * high, 16)] = c[pl.ds(16 * high, 16)]

    def emit(k, value):
        out[k] = value

    edge_rows(index, ext, x, high, emit)


def fill_ext(ext, high, halo, edge, inside, inside_at):
    ext[pl.ds(16 * high, 8)] = halo[...]
    ext[8:16] = edge[...]
    ext[pl.ds(16 - 16 * high, 8)] = inside[pl.ds(inside_at * high, 8)]


def second_edge_kernel(far, index, halo, edge, first, x, after, out, ext):
    high = edge_side(far)
    fill_ext(ext, high, halo, edge, first, 40)

    def emit(k, value):
        out[k] = value

    edge_rows(index, ext, x, high, emit)


def near_kernel(index, halo, edge, mid, x, out, ext):
    high = edge_side(False)
    fill_ext(ext, high, halo, edge, mid, 8)

    def emit(k, value):
        out[k] = value

    edge_rows(index, ext, x, high, emit)


def edge(kernel, *operands):
    return pl.pallas_call(
        kernel,
        out_shape=blocks_of(8),
        in_specs=[VMEM] + [VMEM] * (len(operands) - 1),
        out_specs=VMEM,
        scratch_shapes=[pltpu.VMEM((24, BS, BS), BF)],
        compiler_params=params(4),
        cost_estimate=cost(8, 2 * 2**20),
    )(*operands)


def middle_kernel(
    s_index, v_index, far, near, first, second, layer1, v, s, mid, b0, b1, b2, b3, f, e
):
    place(f, far, near, 0, 40)
    f[8:24] = first[0:16]
    f[24:40] = first[32:48]
    for k in range(8):
        mid[k] = row_product(v[k], f, 0, 8 + k, v_index)
        mid[8 + k] = row_product(v[8 + k], f, 16, 48 + k, v_index)
    e[0:8] = mid[0:8]
    e[8:40] = second[...]
    e[40:48] = mid[8:16]
    _, y, _ = coords()
    for step, out in enumerate((b0, b1, b2, b3)):
        out[0:4] = layer1[4 * step : 4 * step + 4]
        start = layer_start(2, (y + step) % NY)
        slot = stored_slot(2, start)
        for k in range(4):
            out[4 + k] = row_product(s[slot + k], e, 8, start + k, s_index)


def middle(*operands):
    return pl.pallas_call(
        middle_kernel,
        out_shape=[blocks_of(16)] + [blocks_of(8)] * 4,
        in_specs=[VMEM, VMEM] + [VMEM] * 7,
        out_specs=[VMEM] * 5,
        scratch_shapes=[pltpu.VMEM((48, BS, BS), BF), pltpu.VMEM((48, BS, BS), BF)],
        compiler_params=params(4),
        cost_estimate=cost(32, 8 * 2**20),
    )(*operands)


def outer_kernel(index, far, near, mid, second, s, layer3, e):
    place(e, far, near, 0, 40)
    e[8:16] = mid[0:8]
    e[16:24] = second[0:8]
    e[24:32] = second[24:32]
    e[32:40] = mid[8:16]
    _, y, _ = coords()
    for step in range(NY):
        start = layer_start(3, (y + step) % NY)
        slot = stored_slot(3, start)
        base = jnp.where(start < 32, 0, 16)
        for k in range(4):
            layer3[4 * step + k] = row_product(s[slot + k], e, base, start + k, index)


def outer(*operands):
    return pl.pallas_call(
        outer_kernel,
        out_shape=blocks_of(16),
        in_specs=[VMEM] + [VMEM] * 5,
        out_specs=VMEM,
        scratch_shapes=[pltpu.VMEM((48, BS, BS), BF)],
        compiler_params=params(4),
        cost_estimate=cost(16, 4 * 2**20),
    )(*operands)


def last_kernel(
    index, halo, edge, mid, x, near_rows, gaps, layer3, after1, after2, after3, b0, b1, b2, b3, ext, rows
):
    high = edge_side(True)
    rows[pl.ds(8 - 8 * high, 8)] = near_rows[...]
    fill_ext(ext, high, halo, edge, mid, 8)

    def emit(k, value):
        rows[8 * high + k] = value

    edge_rows(index, ext, x, high, emit)
    gap = gaps[...]
    weight = 4.0 * gap / (gap * gap + frequency_sq)
    weighted = (rows[0:2].astype(F32) * weight[None]).astype(BF)
    _, y, _ = coords()
    for step, out in enumerate((b0, b1, b2, b3)):
        out[0:4] = layer3[4 * step : 4 * step + 4]
        out[4:8] = rows[pl.ds(4 * ((y + step) % NY), 4)]
        out[8:10] = weighted


def last(*operands):
    return pl.pallas_call(
        last_kernel,
        out_shape=[blocks_of(10)] * 4,
        in_specs=[VMEM] + [VMEM] * 10,
        out_specs=[VMEM] * 4,
        scratch_shapes=[pltpu.VMEM((24, BS, BS), BF), pltpu.VMEM((16, BS, BS), BF)],
        compiler_params=params(4),
        cost_estimate=cost(8, 4 * 2**20),
    )(*operands)


def chunk(inside, outside, to, half):
    _, y, _ = coords()
    near = jnp.where(to == 2, 0, jnp.where(to == 1, 1, jnp.where(to == 3, 2, 3)))
    away = jnp.where(to == 1, 0, jnp.where(to == 2, 1, jnp.where(to == 0, 2, 3)))
    layer = jnp.where(y < 2, near, away)
    rows = pl.ds(4 * (layer % 2) + 2 * half, 2)
    left = [
        jnp.where(layer < 2, inner_part[rows], outer_part[rows]).reshape(QC, BS)
        for inner_part, outer_part in zip(inside, outside)
    ]
    right = [part[8:10].reshape(QC, BS) for part in outside]
    return lax.dot_general(
        jnp.concatenate(left, axis=1),
        jnp.concatenate(right, axis=1),
        (((1,), (1,)), ((), ())),
        preferred_element_type=F32,
    )


def across_kernel(*refs):
    inside, outside, out = refs[:4], refs[4:8], refs[8]
    x, _, z = coords()
    out[0] = chunk(inside, outside, x, z ^ 1).astype(BF)
    out[1] = chunk(inside, outside, x ^ 2, z ^ 1).astype(BF)


def product_kernel(*refs):
    inside, outside = refs[:4], refs[4:8]
    own, passed, outs = refs[9], refs[10], refs[11:]
    x, _, z = coords()
    for out, (step, flip) in zip(outs, DIRECT):
        out[...] = chunk(inside, outside, (x + step) % NX, z ^ flip).astype(BF)
    passed[...] = chunk(inside, outside, x ^ 2, z)
    own[...] = chunk(inside, outside, x, z)


def product(kernel, tiles, out_shape, *operands):
    return pl.pallas_call(
        kernel,
        out_shape=out_shape,
        in_specs=[VMEM] * len(operands),
        out_specs=jax.tree.map(lambda _: VMEM, out_shape),
        compiler_params=params(8),
        cost_estimate=pl.CostEstimate(
            flops=2 * tiles * QC * QC * 512, bytes_accessed=2**20 * tiles, transcendentals=0
        ),
    )(*operands)


def pass_kernel(passed, arrived, out):
    out[...] = (passed[...] + arrived[1].astype(F32)).astype(BF)


def pass_on(passed, arrived):
    return pl.pallas_call(
        pass_kernel,
        out_shape=jax.ShapeDtypeStruct((QC, QC), BF),
        in_specs=[VMEM] * 2,
        out_specs=VMEM,
        compiler_params=params(4),
        cost_estimate=pl.CostEstimate(flops=QC * QC, bytes_accessed=2**19, transcendentals=0),
    )(passed, arrived)


def add_kernel(own, arrived, *refs):
    total = own[...] + arrived[0].astype(F32)
    for ref in refs[:-1]:
        total += ref[...].astype(F32)
    refs[-1][0] = total


def add_up(*operands):
    return pl.pallas_call(
        add_kernel,
        out_shape=jax.ShapeDtypeStruct((1, QC, QC), F32),
        in_specs=[VMEM] * len(operands),
        out_specs=VMEM,
        compiler_params=params(4),
        cost_estimate=pl.CostEstimate(flops=8 * QC * QC, bytes_accessed=2**20, transcendentals=0),
    )(*operands)


def shift(value, dx, dy, dz):
    pairs = []
    for x in range(NX):
        for y in range(NY):
            for z in range(NZ):
                pairs.append(((x * NY + y) * NZ + z, ((x + dx) % NX * NY + (y ^ dy)) * NZ + (z ^ dz)))
    return lax.ppermute(value, "grp", pairs)


def halo(far, near):
    count = lax.axis_size("sec")
    far_pairs = [(i, (i + 1 if i % 2 else i - 1) % count) for i in range(count)]
    near_pairs = [(i, i ^ 1) for i in range(count)]
    return lax.ppermute(far, "sec", far_pairs), lax.ppermute(near, "sec", near_pairs)


def spread_y(parts, order=(1, 3, 2)):
    out = {0: parts[0]}
    for d in order:
        pairs = []
        for k in range(NX * NY * NZ):
            x, y, z = k // (NY * NZ), k // NZ % NY, k % NZ
            pairs.append((k, (x * NY + (y + d) % NY) * NZ + z))
        out[d] = lax.ppermute(parts[d], "grp", pairs)
    return list(out.values())


def on_device(coefficients, energy_gaps, metric_blocks, metric_index, coulomb_blocks, coulomb_index):
    c = coefficients.reshape(ROWS, BS, BS)
    s, v = metric_blocks, coulomb_blocks
    first_row = lax.axis_index("sec") * ROWS
    s_row, v_row = positions(metric_index, first_row), positions(coulomb_index, first_row)
    gaps = energy_gaps.reshape(1, BS)

    odd = lax.axis_index("sec") % 2 == 1
    c_far, c_near = halo(jnp.where(odd, c[56:], c[:8]), jnp.where(odd, c[:8], c[56:]))
    s_index, v_index, first, second, layer1, *edges_of = inner(s_row, v_row, c, s, v)
    c_edge, s_edge, v_edge, v_mid, s_mid, s_out = edges_of
    first_far, first_near = (functools.partial(first_edge_kernel, far) for far in (True, False))
    second_far, second_near = (functools.partial(second_edge_kernel, far) for far in (True, False))
    f_near = edge(first_near, s_index, c_near, c_edge, s_edge, layer1)
    f_far = edge(first_far, s_index, c_far, c_edge, s_edge, f_near)
    f_far_halo, f_near_halo = halo(f_far, f_near)
    mid, *inside = middle(s_index, v_index, f_far, f_near, first, second, layer1, v_mid, s_mid)
    inside = spread_y(inside)
    e_near = edge(second_near, v_index, f_near_halo, f_near, first, v_edge, mid)
    e_far = edge(second_far, v_index, f_far_halo, f_far, first, v_edge, e_near)
    e_far_halo, e_near_halo = halo(e_far, e_near)
    layer3 = outer(s_index, e_far, e_near, mid, second, s_out)
    b_near = edge(near_kernel, s_index, e_near_halo, e_near, mid, s_edge)
    outside = last(
        s_index, e_far_halo, e_far, mid, s_edge, b_near, gaps, layer3, *inside[1:]
    )
    outside = spread_y(outside)
    tile = jax.ShapeDtypeStruct((QC, QC), BF)
    whole = jax.ShapeDtypeStruct((QC, QC), F32)
    across = product(across_kernel, 2, jax.ShapeDtypeStruct((2, QC, QC), BF), *inside, *outside)
    arrived = shift(across, 0, 0, 1)
    own, passed, *direct = product(
        product_kernel, 6, [whole] * 2 + [tile] * len(DIRECT), *inside, *outside, across
    )
    direct = [shift(part, step, 0, flip) for part, (step, flip) in zip(direct, DIRECT)]
    last_tile = shift(pass_on(passed, arrived), 2, 0, 0)
    return add_up(own, arrived, *direct, last_tile)


def solution(mesh):
    placed = (
        P("sec", "grp"),
        P("grp"),
        P("sec", None, None, None),
        P("sec", None),
        P("sec", None, None, None),
        P("sec", None),
    )
    return jax.shard_map(
        on_device, mesh=mesh, in_specs=placed, out_specs=P("sec", "grp", None), check_vma=False
    )
```
